32 devices in a mesh: groups: 2 (over y), row: 4 (over x, core), col: 4 (over z).
Axes of the slice: x: 2, y: 2, z: 4, core: 2. Of those that a mesh axis runs over, the one named last changes fastest.
Arguments:
- pair_norm: bfloat16 [256, 128, 128], P(('groups', 'row'), 'col'), parts along dimension 0, may hold values from -5 to 5
- pair_rstd: float32 [256, 128], P(('groups', 'row'), 'col'), parts along dimension 0, may hold values from 0.3 to 3
- out_norm: bfloat16 [256, 128, 128], P(('groups', 'row'), 'col'), parts along dimension 0, may hold values from -5 to 5
- out_rstd: float32 [256, 128], P(('groups', 'row'), 'col'), parts along dimension 0, may hold values from 0.3 to 3
- grad_out: bfloat16 [256, 128, 128], P(('groups', 'row'), 'col'), parts along dimension 0, may hold values from -6 to 6
- token_mask: int32 [256], P('groups'), parts along dimension 0, may hold values 0 or 1
- proj_weight: bfloat16 [128, 512], replicated, may hold values from -0.5 to 0.5
- gate_weight: bfloat16 [128, 128], replicated, may hold values from -0.5 to 0.5
- out_weight: bfloat16 [128, 128], replicated, may hold values from -0.5 to 0.5
- out_gain: float32 [128], replicated, may hold values from 0.1 to 1.9
- out_bias: float32 [128], replicated, may hold values from -3 to 3
Outputs:
- pair_grad: float32 [256, 128, 128], P(('groups', 'row'), 'col'), parts along dimension 0
- proj_wgrad: float32 [256, 512], P('groups'), parts along dimension 0
- gate_wgrad: float32 [256, 128], P('groups'), parts along dimension 0
The draws below stay inside these ranges and needn't reach their ends.
There are 2 independent parts, one for each index of `groups`. The reference program is written for one: setup_inputs(seed, part) draws one part's arguments, and reference() takes and returns one part's arrays. A program takes and returns all parts, laid end to end along the dimension named above; an argument that names none is the same for every part. Nothing has to cross between parts.
All inputs are finite; a program needn't handle non-finite values.
Results may differ from the reference program's by a relative error of at most 0.008.
Values may be sent and summed in bfloat16 or wider, within the bound.
A program may use at most 128 MiB of HBM per device.

```python
import math
import jax
import jax.numpy as jnp
from jax import lax

PAIR = 128
HIDDEN_SIZE = 128
TOKENS = 128


def plant(entries, own_key, smallest, high):
    longest = entries.shape.index(max(entries.shape))
    spots = []
    for shift in (0, 1):
        where = [jax.random.randint(jax.random.fold_in(own_key, axis), (), 0, length) for axis, length in enumerate(entries.shape)]
        where[longest] = (where[longest] + shift) % entries.shape[longest]
        spots.append(tuple(where))
    return entries.at[spots[0]].set(smallest).at[spots[1]].set(high)


def block_scale(stream_key, dims, pieces, low, top_value):
    loudness, own = 1.0, jax.random.fold_in(stream_key, 6)
    for axis_at, parts in pieces:
        steps = jnp.exp(jax.random.uniform(jax.random.fold_in(own, axis_at), (parts,), jnp.float32, low / len(pieces), top_value / len(pieces)))
        loudness = loudness * jnp.repeat(steps, dims[axis_at] // parts).reshape([-1 if axis == axis_at else 1 for axis in range(len(dims))])
    return loudness


def bell_draw(rng, shape, scale, most, pieces=(), kind=jnp.bfloat16):
    gain = block_scale(rng, shape, pieces, -0.22, 0.18) if pieces else 1.0
    values = jax.random.normal(rng, shape, jnp.float32) * scale * gain
    return jnp.minimum(jnp.maximum(values, -most), most).astype(kind)


def setup_inputs(seed: int = 0, part: int = 0) -> dict:
    splits = jax.random.split(jax.random.key(seed), 12)
    part_splits = jax.random.split(jax.random.fold_in(splits[11], part), 12)
    return {
        "pair_norm": bell_draw(part_splits[0], (TOKENS, TOKENS, PAIR), 1.0, 5.0, ((0, 4), (1, 4))),
        "pair_rstd": jnp.clip(jnp.exp(math.log(3.0) - 2.3025851 * jax.random.uniform(part_splits[1], (TOKENS, TOKENS), jnp.float32) ** block_scale(part_splits[1], (TOKENS, TOKENS), ((0, 4), (1, 4)), -0.2, 0.2)), 0.3, 3.0),
        "out_norm": bell_draw(part_splits[2], (TOKENS, TOKENS, HIDDEN_SIZE), 1.0, 5.0, ((0, 4), (1, 4))),
        "out_rstd": jnp.clip(jnp.exp(math.log(3.0) - 2.3025851 * jax.random.uniform(part_splits[3], (TOKENS, TOKENS), jnp.float32) ** block_scale(part_splits[3], (TOKENS, TOKENS), ((0, 4), (1, 4)), -0.2, 0.2)), 0.3, 3.0),
        "grad_out": bell_draw(part_splits[4], (TOKENS, TOKENS, PAIR), 1.0, 6.0, ((0, 4), (1, 4))),
        "token_mask": plant((jax.random.randint(part_splits[5], (TOKENS,), 0, 8) < 7).astype(jnp.int32), jax.random.fold_in(part_splits[5], 1), 0, 1),
        "proj_weight": bell_draw(splits[6], (PAIR, 4 * HIDDEN_SIZE), PAIR ** -0.5, 0.5),
        "gate_weight": bell_draw(splits[7], (PAIR, PAIR), PAIR ** -0.5, 0.5),
        "out_weight": bell_draw(splits[8], (HIDDEN_SIZE, PAIR), HIDDEN_SIZE ** -0.5, 0.5),
        "out_gain": jnp.clip(1.0 + 0.18 * jax.random.normal(splits[9], (HIDDEN_SIZE,), jnp.float32), 0.1, 1.9),
        "out_bias": bell_draw(splits[10], (HIDDEN_SIZE,), 0.5, 3.0, (), jnp.float32),
    }


def reference(pair_norm, pair_rstd, out_norm, out_rstd, grad_out, token_mask, proj_weight, gate_weight, out_weight, out_gain, out_bias):
    f32 = jnp.float32
    cells = TOKENS * TOKENS
    flat_norm = pair_norm.reshape(cells, PAIR)
    mask_vals = token_mask.astype(f32)
    pair_mask = (mask_vals[:, None] * mask_vals[None, :])[:, :, None]
    projected = jnp.dot(flat_norm, proj_weight, preferred_element_type=f32).reshape(TOKENS, TOKENS, 4 * HIDDEN_SIZE)
    left_gate = jax.nn.sigmoid(projected[..., :HIDDEN_SIZE])
    left_value = projected[..., HIDDEN_SIZE:2 * HIDDEN_SIZE]
    right_gate = jax.nn.sigmoid(projected[..., 2 * HIDDEN_SIZE:3 * HIDDEN_SIZE])
    right_value = projected[..., 3 * HIDDEN_SIZE:]
    left_proj = (pair_mask * left_gate * left_value).astype(jnp.bfloat16)
    right_proj = (pair_mask * right_gate * right_value).astype(jnp.bfloat16)
    gate_sig = jax.nn.sigmoid(jnp.dot(flat_norm, gate_weight, preferred_element_type=f32))
    hat_out = out_norm.reshape(cells, HIDDEN_SIZE).astype(f32)
    normed_out = (hat_out * out_gain.astype(f32) + out_bias.astype(f32)).astype(jnp.bfloat16)
    update = jnp.dot(normed_out, out_weight, preferred_element_type=f32)
    upstream = grad_out.reshape(cells, PAIR).astype(f32)
    gate_grad = (upstream * update * gate_sig * (1.0 - gate_sig)).astype(jnp.bfloat16)
    update_grad = (upstream * gate_sig).astype(jnp.bfloat16)
    gate_wgrad = lax.dot_general(flat_norm, gate_grad, (((0,), (0,)), ((), ())), preferred_element_type=f32)
    normed_grad = lax.dot_general(update_grad, out_weight, (((1,), (1,)), ((), ())), preferred_element_type=f32) * out_gain.astype(f32)
    tri_grad = out_rstd.reshape(cells, 1).astype(f32) * (normed_grad - jnp.mean(normed_grad, axis=-1, keepdims=True) - hat_out * jnp.mean(normed_grad * hat_out, axis=-1, keepdims=True))
    tri_grad = tri_grad.astype(jnp.bfloat16).reshape(TOKENS, TOKENS, HIDDEN_SIZE).astype(f32)
    left_grad = jnp.einsum('ijh,jkh->ikh', tri_grad, right_proj.astype(f32))
    right_grad = jnp.einsum('ijh,ikh->jkh', tri_grad, left_proj.astype(f32))
    proj_grad = jnp.concatenate([
        left_grad * pair_mask * left_value * left_gate * (1.0 - left_gate),
        left_grad * pair_mask * left_gate,
        right_grad * pair_mask * right_value * right_gate * (1.0 - right_gate),
        right_grad * pair_mask * right_gate], axis=-1).astype(jnp.bfloat16).reshape(cells, 4 * HIDDEN_SIZE)
    proj_wgrad = lax.dot_general(flat_norm, proj_grad, (((0,), (0,)), ((), ())), preferred_element_type=f32)
    norm_grad = lax.dot_general(gate_grad, gate_weight, (((1,), (1,)), ((), ())), preferred_element_type=f32) + lax.dot_general(proj_grad, proj_weight, (((1,), (1,)), ((), ())), preferred_element_type=f32)
    pair_vals = flat_norm.astype(f32)
    pair_grad = pair_rstd.reshape(cells, 1).astype(f32) * (norm_grad - jnp.mean(norm_grad, axis=-1, keepdims=True) - pair_vals * jnp.mean(norm_grad * pair_vals, axis=-1, keepdims=True))
    return pair_grad.reshape(TOKENS, TOKENS, PAIR), proj_wgrad, gate_wgrad
```

```python
import functools

import jax
import jax.numpy as jnp
from jax import lax
from jax.experimental import pallas as pl
from jax.experimental.pallas import tpu as pltpu
from jax.sharding import PartitionSpec as P


def spread(x, axis, root):
    mine = lax.axis_index(axis) == root
    return lax.psum(jnp.where(mine, x, jnp.zeros_like(x)), axis)


def plain(
    pair_norm,
    pair_rstd,
    out_norm,
    out_rstd,
    grad_out,
    token_mask,
    proj_weight,
    gate_weight,
    out_weight,
    out_gain,
    out_bias,
):
    f32 = jnp.float32
    tile_rows, tile_cols, width = pair_norm.shape
    hidden = out_weight.shape[0]
    cells = tile_rows * tile_cols
    col_ratio = lax.axis_size("col") // lax.axis_size("row")
    row_at = lax.axis_index("row")
    col_at = lax.axis_index("col")
    mask_vals = token_mask.astype(f32)
    mask_rows = lax.dynamic_slice_in_dim(mask_vals, row_at * tile_rows, tile_rows)
    mask_cols = lax.dynamic_slice_in_dim(mask_vals, col_at * tile_cols, tile_cols)
    pair_mask = (mask_rows[:, None] * mask_cols[None, :])[:, :, None]
    flat_norm = pair_norm.reshape(cells, width)
    projected = jnp.dot(flat_norm, proj_weight, preferred_element_type=f32).reshape(
        tile_rows, tile_cols, 4 * hidden
    )
    left_gate = jax.nn.sigmoid(projected[..., :hidden])
    left_value = projected[..., hidden : 2 * hidden]
    right_gate = jax.nn.sigmoid(projected[..., 2 * hidden : 3 * hidden])
    right_value = projected[..., 3 * hidden :]
    left_proj = (pair_mask * left_gate * left_value).astype(jnp.bfloat16)
    right_proj = (pair_mask * right_gate * right_value).astype(jnp.bfloat16)
    gate_sig = jax.nn.sigmoid(jnp.dot(flat_norm, gate_weight, preferred_element_type=f32))
    hat_out = out_norm.reshape(cells, hidden).astype(f32)
    normed_out = (hat_out * out_gain + out_bias).astype(jnp.bfloat16)
    update = jnp.dot(normed_out, out_weight, preferred_element_type=f32)
    upstream = grad_out.reshape(cells, width).astype(f32)
    gate_grad = (upstream * update * gate_sig * (1.0 - gate_sig)).astype(jnp.bfloat16)
    update_grad = (upstream * gate_sig).astype(jnp.bfloat16)
    gate_part = lax.dot_general(
        flat_norm, gate_grad, (((0,), (0,)), ((), ())), preferred_element_type=f32
    )
    normed_grad = (
        lax.dot_general(
            update_grad, out_weight, (((1,), (1,)), ((), ())), preferred_element_type=f32
        )
        * out_gain
    )
    tri_grad = out_rstd.reshape(cells, 1) * (
        normed_grad
        - jnp.mean(normed_grad, axis=-1, keepdims=True)
        - hat_out * jnp.mean(normed_grad * hat_out, axis=-1, keepdims=True)
    )
    tri_grad = tri_grad.astype(jnp.bfloat16).reshape(tile_rows, tile_cols, hidden)
    left_cols, right_cols = (
        lax.all_gather(left_proj, "row", axis=0, tiled=True),
        lax.all_gather(right_proj, "row", axis=0, tiled=True),
    )
    left_total = lax.dot_general(
        lax.all_gather(tri_grad, "col", axis=1, tiled=True),
        right_cols,
        (((1,), (0,)), ((2,), (2,))),
        preferred_element_type=f32,
    )
    grad_cols = lax.all_gather(tri_grad, "row", axis=0, tiled=True)
    blocks = []
    for offset in range(col_ratio):
        panel = spread(grad_cols, "col", row_at * col_ratio + offset)
        blocks.append(
            lax.dot_general(
                panel, left_cols, (((0,), (0,)), ((2,), (2,))), preferred_element_type=f32
            )
        )
    right_turned = jnp.concatenate(blocks, axis=1)
    left_grad = jnp.transpose(left_total, (1, 2, 0))
    right_grad = jnp.transpose(right_turned, (1, 2, 0))
    proj_grad = (
        jnp.concatenate(
            [
                left_grad * pair_mask * left_value * left_gate * (1.0 - left_gate),
                left_grad * pair_mask * left_gate,
                right_grad * pair_mask * right_value * right_gate * (1.0 - right_gate),
                right_grad * pair_mask * right_gate,
            ],
            axis=-1,
        )
        .astype(jnp.bfloat16)
        .reshape(cells, 4 * hidden)
    )
    proj_part = lax.dot_general(
        flat_norm, proj_grad, (((0,), (0,)), ((), ())), preferred_element_type=f32
    )
    proj_wgrad, gate_wgrad = lax.psum((proj_part, gate_part), ("row", "col"))
    norm_grad = lax.dot_general(
        gate_grad, gate_weight, (((1,), (1,)), ((), ())), preferred_element_type=f32
    ) + lax.dot_general(
        proj_grad, proj_weight, (((1,), (1,)), ((), ())), preferred_element_type=f32
    )
    pair_vals = flat_norm.astype(f32)
    pair_grad = pair_rstd.reshape(cells, 1) * (
        norm_grad
        - jnp.mean(norm_grad, axis=-1, keepdims=True)
        - pair_vals * jnp.mean(norm_grad * pair_vals, axis=-1, keepdims=True)
    )
    return (pair_grad.reshape(tile_rows, tile_cols, width), proj_wgrad, gate_wgrad)


F32 = jnp.float32
BF16 = jnp.bfloat16
MESH = pl.DeviceIdType.MESH
ROWS_DOT = (((0,), (0,)), ((), ()))
LANES_DOT = (((1,), (1,)), ((), ()))
GROUP = 4


def kernel(
    side,
    tile,
    x_ref,
    pair_rstd_ref,
    hat_ref,
    out_rstd_ref,
    up_ref,
    mask_ref,
    proj_ref,
    gate_ref,
    out_ref,
    gain_ref,
    bias_ref,
    pair_out,
    proj_out,
    gate_out,
    tri_all,
    right_all,
    part_out,
    part_in,
    left32,
    tri32,
    right32,
    left_acc,
    left_a,
    left_b,
    right_a,
    right_b,
    gate_grad,
    proj_grad,
    gate_acc,
    proj_acc,
    w_out,
    w_in,
    w_all,
    tri_send,
    tri_recv,
    right_send,
    right_recv,
    part_send,
    part_recv,
    w_send,
    w_recv,
    all_send,
    all_recv,
):
    row = lax.axis_index("row")
    col = lax.axis_index("col")
    me = row * side + col
    team = side * side
    width = x_ref.shape[-1]
    piece = 4 * width // team
    gate_piece = width // team
    step_rows = 8
    chunks = tile // step_rows
    cells = step_rows * tile

    barrier = pltpu.get_barrier_semaphore()

    def greet(off, carry):
        peer = lax.rem(me + off, team)
        pl.semaphore_signal(
            barrier,
            inc=1,
            device_id={"row": peer // side, "col": lax.rem(peer, side)},
            device_id_type=MESH,
        )
        return carry

    lax.fori_loop(1, team, greet, 0)

    def spot(n):
        return pl.ds(pl.multiple_of(n * cells, cells), cells)

    def lead(n):
        return pl.ds(n * step_rows, step_rows)

    def spread_cells(ref, n):
        part = ref[pl.ds(pl.multiple_of(n * step_rows, step_rows), step_rows), :]
        return jnp.broadcast_to(part[:, :, None], (step_rows, tile, width)).reshape(cells, width)

    gate_acc[...] = jnp.zeros_like(gate_acc)
    proj_acc[...] = jnp.zeros_like(proj_acc)

    def first(n, carry):
        here = spot(n)
        x = x_ref[here, :]
        gate = jax.nn.sigmoid(jnp.dot(x, gate_ref[...], preferred_element_type=F32))
        hat = hat_ref[here, :].astype(F32)
        y = (hat * gain_ref[...] + bias_ref[...]).astype(BF16)
        update = jnp.dot(y, out_ref[...], preferred_element_type=F32)
        up = up_ref[here, :].astype(F32)
        grad = (up * update * gate * (1.0 - gate)).astype(BF16)
        gate_grad[here, :] = grad
        dy = (
            lax.dot_general(
                (up * gate).astype(BF16), out_ref[...], LANES_DOT, preferred_element_type=F32
            )
            * gain_ref[...]
        )
        tri = spread_cells(out_rstd_ref, n) * (
            dy
            - jnp.mean(dy, axis=-1, keepdims=True)
            - hat * jnp.mean(dy * hat, axis=-1, keepdims=True)
        )
        tri_all[col, lead(n)] = tri.astype(BF16).reshape(step_rows, tile, width)
        return carry

    lax.fori_loop(0, chunks, first, 0)
    pl.semaphore_wait(barrier, team - 1)

    def tri_copy(slot, sem, peer):
        return pltpu.make_async_remote_copy(
            src_ref=tri_all.at[slot],
            dst_ref=tri_all.at[slot],
            send_sem=tri_send.at[sem],
            recv_sem=tri_recv.at[slot],
            device_id={"col": peer},
            device_id_type=MESH,
        )

    def right_copy(slot, sem, peer):
        return pltpu.make_async_remote_copy(
            src_ref=right_all.at[slot],
            dst_ref=right_all.at[slot],
            send_sem=right_send.at[sem],
            recv_sem=right_recv.at[slot],
            device_id={"row": peer},
            device_id_type=MESH,
        )

    def part_copy(block, source):
        return pltpu.make_async_remote_copy(
            src_ref=part_out.at[block],
            dst_ref=part_in.at[source],
            send_sem=part_send.at[block],
            recv_sem=part_recv.at[source],
            device_id={"row": block},
            device_id_type=MESH,
        )

    def w_copy(peer, source):
        return pltpu.make_async_remote_copy(
            src_ref=w_out.at[peer],
            dst_ref=w_in.at[source],
            send_sem=w_send.at[peer],
            recv_sem=w_recv.at[source],
            device_id={"row": peer // side, "col": lax.rem(peer, side)},
            device_id_type=MESH,
        )

    def all_copy(peer, source):
        return pltpu.make_async_remote_copy(
            src_ref=w_all.at[source],
            dst_ref=w_all.at[source],
            send_sem=all_send.at[peer],
            recv_sem=all_recv.at[source],
            device_id={"row": peer // side, "col": lax.rem(peer, side)},
            device_id_type=MESH,
        )

    half = col // 2
    turned = col + half * (3 - 2 * col)

    def block_at(s):
        if side != 4:
            return lax.rem(col + s, side)
        t = s if s >= 2 else turned + s * (1 - 2 * turned)
        return t + half * (3 - 2 * t)

    for s in range(1, side):
        tri_copy(col, s, block_at(s)).start()

    col_mask = mask_ref[pl.ds(pl.multiple_of(col * tile, tile), tile), :].astype(F32)

    def second(n, carry):
        here = spot(n)
        proj = jnp.dot(x_ref[here, :], proj_ref[...], preferred_element_type=F32)
        at = pl.multiple_of(row * tile + n * step_rows, step_rows)
        row_mask = mask_ref[pl.ds(at, step_rows), :].astype(F32)
        mask = (row_mask[:, None, :] * col_mask[None, :, :]).reshape(cells, width)
        for base, is_left in ((0, True), (2 * width, False)):
            sig = jax.nn.sigmoid(proj[:, base : base + width])
            value = proj[:, base + width : base + 2 * width]
            open_ = mask * sig
            made = (open_ * value).astype(BF16)
            slope = open_ * value * (1.0 - sig)
            if is_left:
                left32[lead(n)] = made.astype(F32).reshape(step_rows, tile, width)
                left_a[here, :] = slope
                left_b[here, :] = open_
            else:
                right_all[row, lead(n)] = made.reshape(step_rows, tile, width)
                right_a[here, :] = slope
                right_b[here, :] = open_
        return carry

    lax.fori_loop(0, chunks, second, 0)
    for s in range(1, side):
        right_copy(row, s, lax.rem(row + s, side)).start()

    def third(n, carry):
        here = spot(n)
        gate_acc[...] += lax.dot_general(
            x_ref[here, :], gate_grad[here, :], ROWS_DOT, preferred_element_type=F32
        )
        return carry

    lax.fori_loop(0, chunks, third, 0)

    for s in range(side):
        block = block_at(s)
        if s > 0:
            tri_copy(block, 0, block).wait_recv()
        tri32[...] = tri_all[block].astype(F32)

        def part_step(g, carry, block=block):
            at = g * GROUP
            sums = [None] * GROUP
            for i in range(tile):
                mine = left32[i]
                for q in range(GROUP):
                    term = tri32[i, pl.ds(at + q, 1), :] * mine
                    sums[q] = term if sums[q] is None else sums[q] + term
            for q in range(GROUP):
                part_out[block, at + q] = sums[q].astype(BF16)
            return carry

        lax.fori_loop(0, tile // GROUP, part_step, 0)

        @pl.when(block != row)
        def _(block=block):
            part_copy(block, row).start()
            right_copy(block, 0, block).wait_recv()

        @pl.when(block == row)
        def _(block=block):
            part_in[row] = part_out[block]

        right32[...] = right_all[block].astype(F32)

        def left_step(g, carry, s=s):
            at = g * GROUP
            sums = [None if s == 0 else left_acc[at + q] for q in range(GROUP)]
            for j in range(tile):
                mine = right32[j]
                for q in range(GROUP):
                    term = tri32[at + q, pl.ds(j, 1), :] * mine
                    sums[q] = term if sums[q] is None else sums[q] + term
            for q in range(GROUP):
                left_acc[at + q] = sums[q]
            return carry

        lax.fori_loop(0, tile // GROUP, left_step, 0)

    for s in range(1, side):
        part_copy(row, lax.rem(row + s, side)).wait_recv()

    def fourth(n, carry):
        here = spot(n)
        left_grad = left_acc[lead(n)].reshape(cells, width)
        right_grad = part_in[0, lead(n)].astype(F32)
        for r in range(1, side):
            right_grad = right_grad + part_in[r, lead(n)].astype(F32)
        right_grad = right_grad.reshape(cells, width)
        x = x_ref[here, :]
        for q, grad in enumerate(
            (
                left_grad * left_a[here, :],
                left_grad * left_b[here, :],
                right_grad * right_a[here, :],
                right_grad * right_b[here, :],
            )
        ):
            grad = grad.astype(BF16)
            proj_grad[here, q * width : (q + 1) * width] = grad
            proj_acc[q * width : (q + 1) * width, :] += lax.dot_general(
                x, grad, ROWS_DOT, preferred_element_type=F32
            )
        return carry

    lax.fori_loop(0, chunks, fourth, 0)

    pad = piece + 16
    w_out[:, 0:piece, :] = proj_acc[...].reshape(team, piece, width).astype(BF16)
    own_gate = gate_acc[...].reshape(team, gate_piece, width)
    w_out[:, piece:pad, :] = jnp.concatenate(
        [own_gate, jnp.zeros((team, 16 - gate_piece, width), F32)], axis=1
    ).astype(BF16)

    def send_piece(off, carry):
        w_copy(lax.rem(me + off, team), me).start()
        return carry

    lax.fori_loop(1, team, send_piece, 0)
    w_in[me] = w_out[me]

    def fifth(n, carry):
        here = spot(n)
        grad = lax.dot_general(
            gate_grad[here, :], gate_ref[...], LANES_DOT, preferred_element_type=F32
        ) + lax.dot_general(
            proj_grad[here, :], proj_ref[...], LANES_DOT, preferred_element_type=F32
        )
        x = x_ref[here, :].astype(F32)
        pair_out[here, :] = spread_cells(pair_rstd_ref, n) * (
            grad
            - jnp.mean(grad, axis=-1, keepdims=True)
            - x * jnp.mean(grad * x, axis=-1, keepdims=True)
        )
        return carry

    lax.fori_loop(0, chunks, fifth, 0)

    def get_piece(off, carry):
        w_copy(me, lax.rem(me + off, team)).wait_recv()
        return carry

    lax.fori_loop(1, team, get_piece, 0)
    total = w_in[0].astype(F32)
    for p in range(1, team):
        total = total + w_in[p].astype(F32)
    w_all[me] = total.astype(BF16)

    def send_total(off, carry):
        all_copy(lax.rem(me + off, team), me).start()
        return carry

    lax.fori_loop(1, team, send_total, 0)

    for s in range(1, side):
        tri_copy(col, s, block_at(s)).wait_send()
        right_copy(row, s, lax.rem(row + s, side)).wait_send()
        part_copy(lax.rem(row + s, side), row).wait_send()

    def finish(off, carry):
        w_copy(lax.rem(me + off, team), me).wait_send()
        return carry

    lax.fori_loop(1, team, finish, 0)

    def get_total(off, carry):
        peer = lax.rem(me + off, team)
        all_copy(me, peer).wait_recv()
        return carry

    lax.fori_loop(1, team, get_total, 0)

    def finish_total(off, carry):
        all_copy(lax.rem(me + off, team), me).wait_send()
        return carry

    lax.fori_loop(1, team, finish_total, 0)

    each = width // piece
    for q in range(4):
        proj_out[:, q * width : (q + 1) * width] = (
            w_all[q * each : (q + 1) * each, 0:piece, :].astype(F32).reshape(width, width)
        )
    gate_out[...] = w_all[:, piece:pad, :].astype(F32)[:, 0:gate_piece, :].reshape(width, width)


def fused(
    pair_norm,
    pair_rstd,
    out_norm,
    out_rstd,
    grad_out,
    token_mask,
    proj_weight,
    gate_weight,
    out_weight,
    out_gain,
    out_bias,
):
    tile, _, width = pair_norm.shape
    side = lax.axis_size("row")
    team = side * side
    cells = tile * tile
    piece = 4 * width // team + 16
    vmem = pl.BlockSpec(memory_space=pltpu.VMEM)
    dma = pltpu.SemaphoreType.DMA
    tokens = token_mask.shape[0]
    mask = jnp.broadcast_to(token_mask[:, None], (tokens, width))
    pair_grad, proj_wgrad, gate_wgrad = pl.pallas_call(
        functools.partial(kernel, side, tile),
        out_shape=(
            jax.ShapeDtypeStruct((cells, width), F32),
            jax.ShapeDtypeStruct((width, 4 * width), F32),
            jax.ShapeDtypeStruct((width, width), F32),
        ),
        in_specs=[vmem] * 11,
        out_specs=(vmem, vmem, vmem),
        scratch_shapes=[
            pltpu.VMEM((side, tile, tile, width), BF16),
            pltpu.VMEM((side, tile, tile, width), BF16),
            pltpu.VMEM((side, tile, tile, width), BF16),
            pltpu.VMEM((side, tile, tile, width), BF16),
            pltpu.VMEM((tile, tile, width), F32),
            pltpu.VMEM((tile, tile, width), F32),
            pltpu.VMEM((tile, tile, width), F32),
            pltpu.VMEM((tile, tile, width), F32),
            pltpu.VMEM((cells, width), F32),
            pltpu.VMEM((cells, width), F32),
            pltpu.VMEM((cells, width), F32),
            pltpu.VMEM((cells, width), F32),
            pltpu.VMEM((cells, width), BF16),
            pltpu.VMEM((cells, 4 * width), BF16),
            pltpu.VMEM((width, width), F32),
            pltpu.VMEM((4 * width, width), F32),
            pltpu.VMEM((team, piece, width), BF16),
            pltpu.VMEM((team, piece, width), BF16),
            pltpu.VMEM((team, piece, width), BF16),
            dma((side,)),
            dma((side,)),
            dma((side,)),
            dma((side,)),
            dma((side,)),
            dma((side,)),
            dma((team,)),
            dma((team,)),
            dma((team,)),
            dma((team,)),
        ],
        compiler_params=pltpu.CompilerParams(
            collective_id=0, has_side_effects=True, vmem_limit_bytes=40 * 1024 * 1024
        ),
    )(
        pair_norm.reshape(cells, width),
        pair_rstd,
        out_norm.reshape(cells, width),
        out_rstd,
        grad_out.reshape(cells, width),
        mask,
        proj_weight,
        gate_weight,
        out_weight,
        out_gain.reshape(1, width),
        out_bias.reshape(1, width),
    )
    return pair_grad.reshape(tile, tile, width), proj_wgrad, gate_wgrad


def local(pair_norm, *rest):
    rows, cols = lax.axis_size("row"), lax.axis_size("col")
    tile_rows, tile_cols, width = pair_norm.shape
    hidden = rest[7].shape[0]
    team = rows * cols
    fits = (
        rows == cols
        and tile_rows == tile_cols
        and tile_rows % 16 == 0
        and tile_rows <= 32
        and hidden == width
        and width == 128
        and 8 <= team <= 32
        and width % team == 0
        and 4 * width // team % 16 == 0
    )
    return (fused if fits else plain)(pair_norm, *rest)


def solution(mesh):
    placed = (
        P(("groups", "row"), "col", None),
        P(("groups", "row"), "col"),
        P(("groups", "row"), "col", None),
        P(("groups", "row"), "col"),
        P(("groups", "row"), "col", None),
        P("groups"),
        P(),
        P(),
        P(),
        P(),
        P(),
    )
    return jax.shard_map(
        local,
        mesh=mesh,
        in_specs=placed,
        out_specs=(P(("groups", "row"), "col", None), P("groups", None), P("groups", None)),
        check_vma=False,
    )
```

```python
import functools

import jax
import jax.numpy as jnp
from jax import lax
from jax.experimental import pallas as pl
from jax.experimental.pallas import tpu as pltpu
from jax.sharding import PartitionSpec as P


def spread(x, axis, root):
    mine = lax.axis_index(axis) == root
    return lax.psum(jnp.where(mine, x, jnp.zeros_like(x)), axis)


def plain(
    pair_norm,
    pair_rstd,
    out_norm,
    out_rstd,
    grad_out,
    token_mask,
    proj_weight,
    gate_weight,
    out_weight,
    out_gain,
    out_bias,
):
    f32 = jnp.float32
    tile_rows, tile_cols, width = pair_norm.shape
    hidden = out_weight.shape[0]
    cells = tile_rows * tile_cols
    col_ratio = lax.axis_size("col") // lax.axis_size("row")
    row_at = lax.axis_index("row")
    col_at = lax.axis_index("col")
    mask_vals = token_mask.astype(f32)
    mask_rows = lax.dynamic_slice_in_dim(mask_vals, row_at * tile_rows, tile_rows)
    mask_cols = lax.dynamic_slice_in_dim(mask_vals, col_at * tile_cols, tile_cols)
    pair_mask = (mask_rows[:, None] * mask_cols[None, :])[:, :, None]
    flat_norm = pair_norm.reshape(cells, width)
    projected = jnp.dot(flat_norm, proj_weight, preferred_element_type=f32).reshape(
        tile_rows, tile_cols, 4 * hidden
    )
    left_gate = jax.nn.sigmoid(projected[..., :hidden])
    left_value = projected[..., hidden : 2 * hidden]
    right_gate = jax.nn.sigmoid(projected[..., 2 * hidden : 3 * hidden])
    right_value = projected[..., 3 * hidden :]
    left_proj = (pair_mask * left_gate * left_value).astype(jnp.bfloat16)
    right_proj = (pair_mask * right_gate * right_value).astype(jnp.bfloat16)
    gate_sig = jax.nn.sigmoid(jnp.dot(flat_norm, gate_weight, preferred_element_type=f32))
    hat_out = out_norm.reshape(cells, hidden).astype(f32)
    normed_out = (hat_out * out_gain + out_bias).astype(jnp.bfloat16)
    update = jnp.dot(normed_out, out_weight, preferred_element_type=f32)
    upstream = grad_out.reshape(cells, width).astype(f32)
    gate_grad = (upstream * update * gate_sig * (1.0 - gate_sig)).astype(jnp.bfloat16)
    update_grad = (upstream * gate_sig).astype(jnp.bfloat16)
    gate_part = lax.dot_general(
        flat_norm, gate_grad, (((0,), (0,)), ((), ())), preferred_element_type=f32
    )
    normed_grad = (
        lax.dot_general(
            update_grad, out_weight, (((1,), (1,)), ((), ())), preferred_element_type=f32
        )
        * out_gain
    )
    tri_grad = out_rstd.reshape(cells, 1) * (
        normed_grad
        - jnp.mean(normed_grad, axis=-1, keepdims=True)
        - hat_out * jnp.mean(normed_grad * hat_out, axis=-1, keepdims=True)
    )
    tri_grad = tri_grad.astype(jnp.bfloat16).reshape(tile_rows, tile_cols, hidden)
    left_cols, right_cols = (
        lax.all_gather(left_proj, "row", axis=0, tiled=True),
        lax.all_gather(right_proj, "row", axis=0, tiled=True),
    )
    left_total = lax.dot_general(
        lax.all_gather(tri_grad, "col", axis=1, tiled=True),
        right_cols,
        (((1,), (0,)), ((2,), (2,))),
        preferred_element_type=f32,
    )
    grad_cols = lax.all_gather(tri_grad, "row", axis=0, tiled=True)
    blocks = []
    for offset in range(col_ratio):
        panel = spread(grad_cols, "col", row_at * col_ratio + offset)
        blocks.append(
            lax.dot_general(
                panel, left_cols, (((0,), (0,)), ((2,), (2,))), preferred_element_type=f32
            )
        )
    right_turned = jnp.concatenate(blocks, axis=1)
    left_grad = jnp.transpose(left_total, (1, 2, 0))
    right_grad = jnp.transpose(right_turned, (1, 2, 0))
    proj_grad = (
        jnp.concatenate(
            [
                left_grad * pair_mask * left_value * left_gate * (1.0 - left_gate),
                left_grad * pair_mask * left_gate,
                right_grad * pair_mask * right_value * right_gate * (1.0 - right_gate),
                right_grad * pair_mask * right_gate,
            ],
            axis=-1,
        )
        .astype(jnp.bfloat16)
        .reshape(cells, 4 * hidden)
    )
    proj_part = lax.dot_general(
        flat_norm, proj_grad, (((0,), (0,)), ((), ())), preferred_element_type=f32
    )
    proj_wgrad, gate_wgrad = lax.psum((proj_part, gate_part), ("row", "col"))
    norm_grad = lax.dot_general(
        gate_grad, gate_weight, (((1,), (1,)), ((), ())), preferred_element_type=f32
    ) + lax.dot_general(
        proj_grad, proj_weight, (((1,), (1,)), ((), ())), preferred_element_type=f32
    )
    pair_vals = flat_norm.astype(f32)
    pair_grad = pair_rstd.reshape(cells, 1) * (
        norm_grad
        - jnp.mean(norm_grad, axis=-1, keepdims=True)
        - pair_vals * jnp.mean(norm_grad * pair_vals, axis=-1, keepdims=True)
    )
    return (pair_grad.reshape(tile_rows, tile_cols, width), proj_wgrad, gate_wgrad)


F32 = jnp.float32
BF16 = jnp.bfloat16
MESH = pl.DeviceIdType.MESH
ROWS_DOT = (((0,), (0,)), ((), ()))
LANES_DOT = (((1,), (1,)), ((), ()))
GROUP = 4


def kernel(
    side,
    tile,
    x_hbm,
    pair_rstd_hbm,
    hat_hbm,
    out_rstd_hbm,
    up_hbm,
    mask_hbm,
    proj_hbm,
    gate_hbm,
    out_hbm,
    gain_hbm,
    bias_hbm,
    pair_out,
    proj_out,
    gate_out,
    x_ref,
    pair_rstd_ref,
    hat_ref,
    out_rstd_ref,
    up_ref,
    mask_in,
    proj_ref,
    gate_ref,
    out_ref,
    gain_ref,
    bias_ref,
    mask_ref,
    tri_all,
    right_all,
    part_out,
    part_in,
    relay_in,
    left32,
    tri32,
    right32,
    left_acc,
    left_a,
    left_b,
    right_a,
    right_b,
    gate_grad,
    proj_grad,
    gate_acc,
    proj_acc,
    w_out,
    w_in,
    w_all,
    load_sem,
    tri_send,
    tri_recv,
    right_send,
    right_recv,
    part_send,
    part_recv,
    relay_recv,
    w_send,
    w_recv,
    all_send,
    all_recv,
):
    loads = [
        pltpu.make_async_copy(source, target, load_sem.at[k])
        for k, (source, target) in enumerate(
            (
                (x_hbm, x_ref),
                (hat_hbm, hat_ref),
                (up_hbm, up_ref),
                (gate_hbm, gate_ref),
                (out_hbm, out_ref),
                (out_rstd_hbm, out_rstd_ref),
                (gain_hbm, gain_ref),
                (bias_hbm, bias_ref),
                (mask_hbm, mask_in),
                (proj_hbm, proj_ref),
                (pair_rstd_hbm, pair_rstd_ref),
            )
        )
    ]
    for load in loads:
        load.start()

    row = lax.axis_index("row")
    col = lax.axis_index("col")
    me = row * side + col
    team = side * side
    width = x_ref.shape[-1]
    step_rows = 8
    chunks = tile // step_rows
    cells = step_rows * tile
    part = tile // 2
    sibling = row + 1 - 2 * lax.rem(row, 2)
    across = lax.rem(row + 2, side)
    beyond = lax.rem(sibling + 2, side)

    barrier = pltpu.get_barrier_semaphore()

    def place(peer):
        return {"row": peer // side, "col": lax.rem(peer, side)}

    def greet(off, carry):
        pl.semaphore_signal(
            barrier, inc=1, device_id=place(lax.rem(me + off, team)), device_id_type=MESH
        )
        return carry

    lax.fori_loop(1, team, greet, 0)

    def spot(n):
        return pl.ds(pl.multiple_of(n * cells, cells), cells)

    def lead(n):
        return pl.ds(n * step_rows, step_rows)

    def spread_cells(ref, n):
        rows = ref[pl.ds(pl.multiple_of(n * step_rows, step_rows), step_rows), :]
        return jnp.broadcast_to(rows[:, :, None], (step_rows, tile, width)).reshape(cells, width)

    def remote(source, target, send, recv, where):
        return pltpu.make_async_remote_copy(
            src_ref=source,
            dst_ref=target,
            send_sem=send,
            recv_sem=recv,
            device_id=where,
            device_id_type=MESH,
        )

    def tri_copy(slot, h, sem, peer):
        piece = tri_all.at[slot, :, pl.ds(h * part, part), :]
        return remote(piece, piece, tri_send.at[sem, h], tri_recv.at[slot, h], {"col": peer})

    def right_copy(slot, sem, peer):
        return remote(
            right_all.at[slot],
            right_all.at[slot],
            right_send.at[sem],
            right_recv.at[slot],
            {"row": peer},
        )

    def part_copy(block, h, kind, peer):
        here = pl.ds(h * part, part)
        return remote(
            part_out.at[block, here],
            part_in.at[kind, here],
            part_send.at[block, h],
            part_recv.at[kind, h],
            {"row": peer},
        )

    def relay_copy(block, h):
        here = pl.ds(h * part, part)
        return remote(
            part_out.at[block, here],
            relay_in.at[here],
            part_send.at[block, h],
            relay_recv.at[h],
            {"row": sibling},
        )

    def w_copy(k, peer, source):
        return remote(
            w_out.at[k, peer],
            w_in.at[k, source],
            w_send.at[k, peer],
            w_recv.at[k, source],
            place(peer),
        )

    def all_copy(k, peer, source):
        return remote(
            w_all.at[k, source],
            w_all.at[k, source],
            all_send.at[k, peer],
            all_recv.at[k, source],
            place(peer),
        )

    gate_acc[...] = jnp.zeros_like(gate_acc)
    proj_acc[...] = jnp.zeros_like(proj_acc)
    for load in loads[:8]:
        load.wait()

    def first(n, carry):
        here = spot(n)
        x = x_ref[here, :]
        gate = jax.nn.sigmoid(jnp.dot(x, gate_ref[...], preferred_element_type=F32))
        hat = hat_ref[here, :].astype(F32)
        y = (hat * gain_ref[...] + bias_ref[...]).astype(BF16)
        update = jnp.dot(y, out_ref[...], preferred_element_type=F32)
        up = up_ref[here, :].astype(F32)
        grad = (up * update * gate * (1.0 - gate)).astype(BF16)
        gate_grad[here, :] = grad
        dy = (
            lax.dot_general(
                (up * gate).astype(BF16), out_ref[...], LANES_DOT, preferred_element_type=F32
            )
            * gain_ref[...]
        )
        tri = spread_cells(out_rstd_ref, n) * (
            dy
            - jnp.mean(dy, axis=-1, keepdims=True)
            - hat * jnp.mean(dy * hat, axis=-1, keepdims=True)
        )
        tri_all[col, lead(n)] = tri.astype(BF16).reshape(step_rows, tile, width)
        return carry

    lax.fori_loop(0, chunks, first, 0)
    for load in loads[8:]:
        load.wait()
    pl.semaphore_wait(barrier, team - 1)

    upper = col // 2
    inner = lax.rem(col + upper, 2)

    def mirror(t):
        return t + upper * (3 - 2 * t)

    def block_at(s):
        return mirror(s if s >= 2 else inner + s * (1 - 2 * inner))

    toward_end, toward_middle = mirror(0), mirror(inner + 1)

    for h in range(2):
        tri_copy(col, h, 0, toward_middle).start()

        @pl.when(inner == 1)
        def _(h=h):
            tri_copy(col, h, 1, toward_end).start()

    def forward_to(s):
        return toward_middle if s == 1 else toward_end

    def take_tri(s, h):
        block = block_at(s)
        tri_copy(block, h, 0, block).wait_recv()

        @pl.when(inner == 1)
        def _():
            tri_copy(block, h, s + 1, forward_to(s)).start()

    mask_ref[...] = jnp.transpose(
        jnp.broadcast_to(mask_in[...].astype(F32), (width, mask_in.shape[-1]))
    )
    col_mask = mask_ref[pl.ds(pl.multiple_of(col * tile, tile), tile), :]

    def second(n, carry):
        here = spot(n)
        proj = jnp.dot(x_ref[here, :], proj_ref[...], preferred_element_type=F32)
        at = pl.multiple_of(row * tile + n * step_rows, step_rows)
        row_mask = mask_ref[pl.ds(at, step_rows), :]
        mask = (row_mask[:, None, :] * col_mask[None, :, :]).reshape(cells, width)
        for base, is_left in ((0, True), (2 * width, False)):
            sig = jax.nn.sigmoid(proj[:, base : base + width])
            value = proj[:, base + width : base + 2 * width]
            open_ = mask * sig
            made = (open_ * value).astype(BF16)
            slope = open_ * value * (1.0 - sig)
            if is_left:
                left32[lead(n)] = made.astype(F32).reshape(step_rows, tile, width)
                left_a[here, :] = slope
                left_b[here, :] = open_
            else:
                right_all[row, lead(n)] = made.reshape(step_rows, tile, width)
                right_a[here, :] = slope
                right_b[here, :] = open_
        return carry

    lax.fori_loop(0, chunks, second, 0)
    right_copy(row, 0, across).start()
    right_copy(row, 1, sibling).start()

    def do_part(s, h):
        block = block_at(s)
        span = pl.ds(h * part, part)
        tri32[:, span, :] = tri_all[block, :, span, :].astype(F32)

        def body(g, carry):
            at = h * part + g * GROUP
            sums = [None] * GROUP
            for i in range(tile):
                mine = left32[i]
                for q in range(GROUP):
                    term = tri32[i, pl.ds(at + q, 1), :] * mine
                    sums[q] = term if sums[q] is None else sums[q] + term
            for q in range(GROUP):
                part_out[block, at + q] = sums[q].astype(BF16)
            return carry

        lax.fori_loop(0, part // GROUP, body, 0)

        @pl.when(block == sibling)
        def _():
            part_copy(block, h, 0, sibling).start()

        @pl.when(block == beyond)
        def _():
            relay_copy(block, h).start()

    def do_relay(s, h):
        block = block_at(s)
        span = pl.ds(h * part, part)

        @pl.when(block == across)
        def _():
            relay_copy(block, h).wait_recv()
            part_out[block, span] = (
                part_out[block, span].astype(F32) + relay_in[span].astype(F32)
            ).astype(BF16)
            part_copy(block, h, 1, across).start()

    def do_left(s):
        block = block_at(s)
        right32[...] = right_all[block].astype(F32)

        def body(g, carry):
            at = g * GROUP
            sums = [None if s == 0 else left_acc[at + q] for q in range(GROUP)]
            for j in range(tile):
                mine = right32[j]
                for q in range(GROUP):
                    term = tri32[at + q, pl.ds(j, 1), :] * mine
                    sums[q] = term if sums[q] is None else sums[q] + term
            for q in range(GROUP):
                left_acc[at + q] = sums[q]
            return carry

        lax.fori_loop(0, tile // GROUP, body, 0)

    for h in range(2):
        do_part(0, h)

    def third(n, carry):
        here = spot(n)
        gate_acc[...] += lax.dot_general(
            x_ref[here, :], gate_grad[here, :], ROWS_DOT, preferred_element_type=F32
        )
        return carry

    lax.fori_loop(0, chunks, third, 0)
    for h in range(2):
        do_relay(0, h)
    for h in range(2):
        take_tri(1, h)
    right_copy(across, 0, across).wait_recv()
    right_copy(across, 2, sibling).start()
    right_copy(sibling, 0, sibling).wait_recv()
    right_copy(beyond, 0, sibling).wait_recv()
    do_left(0)
    for s in range(1, side):
        for h in range(2):
            if s > 1:
                take_tri(s, h)
            do_part(s, h)
        if s < side - 1:
            do_left(s)
        for h in range(2):
            do_relay(s, h)
        if s == side - 1:
            do_left(s)

    def weights(n, grads, base):
        here = spot(n)
        x = x_ref[here, :]
        for q, grad in enumerate(grads):
            grad = grad.astype(BF16)
            at = (base + q) * width
            proj_grad[here, at : at + width] = grad
            proj_acc[at : at + width, :] += lax.dot_general(
                x, grad, ROWS_DOT, preferred_element_type=F32
            )

    def left_weights(n, carry):
        here = spot(n)
        grad = left_acc[lead(n)].reshape(cells, width)
        weights(n, (grad * left_a[here, :], grad * left_b[here, :]), 0)
        return carry

    def right_weights(n, carry):
        here = spot(n)
        grad = part_out[row, lead(n)].astype(F32)
        for kind in range(2):
            grad = grad + part_in[kind, lead(n)].astype(F32)
        grad = grad.reshape(cells, width)
        weights(n, (grad * right_a[here, :], grad * right_b[here, :]), 2)
        return carry

    piece = 2 * width // team
    gate_piece = width // team

    def send_pieces(k):
        half = proj_acc[2 * k * width : 2 * (k + 1) * width, :]
        w_out[k, :, 0:piece, :] = half.reshape(team, piece, width).astype(BF16)

        def body(off, carry):
            w_copy(k, lax.rem(me + off, team), me).start()
            return carry

        lax.fori_loop(1, team, body, 0)
        w_in[k, me] = w_out[k, me]

    def send_totals(k):
        def body(off, carry):
            w_copy(k, me, lax.rem(me + off, team)).wait_recv()
            return carry

        lax.fori_loop(1, team, body, 0)
        total = w_in[k, 0].astype(F32)
        for p in range(1, team):
            total = total + w_in[k, p].astype(F32)
        w_all[k, me] = total.astype(BF16)

        def push(off, carry):
            all_copy(k, lax.rem(me + off, team), me).start()
            return carry

        lax.fori_loop(1, team, push, 0)

    lax.fori_loop(0, chunks, left_weights, 0)
    w_out[0, :, piece : piece + 16, :] = jnp.concatenate(
        [
            gate_acc[...].reshape(team, gate_piece, width),
            jnp.zeros((team, 16 - gate_piece, width), F32),
        ],
        axis=1,
    ).astype(BF16)
    w_out[1, :, piece : piece + 16, :] = jnp.zeros((team, 16, width), BF16)
    send_pieces(0)
    for kind in range(2):
        for h in range(2):
            part_copy(row, h, kind, sibling).wait_recv()
    lax.fori_loop(0, chunks, right_weights, 0)
    send_pieces(1)
    send_totals(0)

    def last(n, carry):
        here = spot(n)
        grad = lax.dot_general(
            gate_grad[here, :], gate_ref[...], LANES_DOT, preferred_element_type=F32
        ) + lax.dot_general(
            proj_grad[here, :], proj_ref[...], LANES_DOT, preferred_element_type=F32
        )
        x = x_ref[here, :].astype(F32)
        pair_out[here, :] = spread_cells(pair_rstd_ref, n) * (
            grad
            - jnp.mean(grad, axis=-1, keepdims=True)
            - x * jnp.mean(grad * x, axis=-1, keepdims=True)
        )
        return carry

    lax.fori_loop(0, chunks // 2, last, 0)
    send_totals(1)
    lax.fori_loop(chunks // 2, chunks, last, 0)

    for h in range(2):
        tri_copy(col, h, 0, toward_middle).wait_send()

        @pl.when(inner == 1)
        def _(h=h):
            tri_copy(col, h, 1, toward_end).wait_send()
            for s in range(1, side):
                tri_copy(block_at(s), h, s + 1, forward_to(s)).wait_send()

        part_copy(sibling, h, 0, sibling).wait_send()
        relay_copy(beyond, h).wait_send()
        part_copy(across, h, 1, across).wait_send()
    right_copy(row, 0, across).wait_send()
    right_copy(row, 1, sibling).wait_send()
    right_copy(across, 2, sibling).wait_send()

    def finish(off, carry):
        peer = lax.rem(me + off, team)
        for k in range(2):
            w_copy(k, peer, me).wait_send()
        return carry

    lax.fori_loop(1, team, finish, 0)

    def get_totals(off, carry):
        peer = lax.rem(me + off, team)
        for k in range(2):
            all_copy(k, me, peer).wait_recv()
        return carry

    lax.fori_loop(1, team, get_totals, 0)

    def finish_totals(off, carry):
        peer = lax.rem(me + off, team)
        for k in range(2):
            all_copy(k, peer, me).wait_send()
        return carry

    lax.fori_loop(1, team, finish_totals, 0)

    each = width // piece
    for q in range(4):
        k, at = q // 2, (q % 2) * each
        proj_out[:, q * width : (q + 1) * width] = (
            w_all[k, at : at + each, 0:piece, :].astype(F32).reshape(width, width)
        )
    gate_out[...] = (
        w_all[0, :, piece : piece + 16, :].astype(F32)[:, 0:gate_piece, :].reshape(width, width)
    )


def flush(*refs):
    count = len(refs) // 3
    sources, targets, held = refs[:count], refs[count : 2 * count], refs[2 * count : -1]
    sem = refs[-1]
    reads = [
        pltpu.make_async_copy(sources[k], held[k], sem.at[0, k]) for k in range(count)
    ]
    writes = [
        pltpu.make_async_copy(held[k], targets[k], sem.at[1, k]) for k in range(count)
    ]
    for read in reads:
        read.start()
    for read, write in zip(reads, writes):
        read.wait()
        write.start()
    for write in writes:
        write.wait()


def fused(
    pair_norm,
    pair_rstd,
    out_norm,
    out_rstd,
    grad_out,
    token_mask,
    proj_weight,
    gate_weight,
    out_weight,
    out_gain,
    out_bias,
):
    tile, _, width = pair_norm.shape
    side = lax.axis_size("row")
    team = side * side
    cells = tile * tile
    piece = 2 * width // team + 16
    tokens = token_mask.shape[0]
    vmem = pl.BlockSpec(memory_space=pltpu.VMEM)
    hbm = pl.BlockSpec(memory_space=pltpu.HBM)
    dma = pltpu.SemaphoreType.DMA
    shapes = (
        jax.ShapeDtypeStruct((cells, width), F32),
        jax.ShapeDtypeStruct((width, 4 * width), F32),
        jax.ShapeDtypeStruct((width, width), F32),
    )
    arrays = (
        pair_norm.reshape(cells, width),
        pair_rstd,
        out_norm.reshape(cells, width),
        out_rstd,
        grad_out.reshape(cells, width),
        token_mask.reshape(1, tokens),
        proj_weight,
        gate_weight,
        out_weight,
        out_gain.reshape(1, width),
        out_bias.reshape(1, width),
    )
    made = pl.pallas_call(
        functools.partial(kernel, side, tile),
        out_shape=shapes,
        in_specs=[hbm] * 11,
        out_specs=(vmem, vmem, vmem),
        scratch_shapes=[pltpu.VMEM(a.shape, a.dtype) for a in arrays]
        + [
            pltpu.VMEM((tokens, width), F32),
            pltpu.VMEM((side, tile, tile, width), BF16),
            pltpu.VMEM((side, tile, tile, width), BF16),
            pltpu.VMEM((side, tile, tile, width), BF16),
            pltpu.VMEM((2, tile, tile, width), BF16),
            pltpu.VMEM((tile, tile, width), BF16),
            pltpu.VMEM((tile, tile, width), F32),
            pltpu.VMEM((tile, tile, width), F32),
            pltpu.VMEM((tile, tile, width), F32),
            pltpu.VMEM((tile, tile, width), F32),
            pltpu.VMEM((cells, width), F32),
            pltpu.VMEM((cells, width), F32),
            pltpu.VMEM((cells, width), F32),
            pltpu.VMEM((cells, width), F32),
            pltpu.VMEM((cells, width), BF16),
            pltpu.VMEM((cells, 4 * width), BF16),
            pltpu.VMEM((width, width), F32),
            pltpu.VMEM((4 * width, width), F32),
            pltpu.VMEM((2, team, piece, width), BF16),
            pltpu.VMEM((2, team, piece, width), BF16),
            pltpu.VMEM((2, team, piece, width), BF16),
            dma((11,)),
            dma((side + 1, 2)),
            dma((side, 2)),
            dma((side,)),
            dma((side,)),
            dma((side, 2)),
            dma((2, 2)),
            dma((2,)),
            dma((2, team)),
            dma((2, team)),
            dma((2, team)),
            dma((2, team)),
        ],
        compiler_params=pltpu.CompilerParams(
            collective_id=0, has_side_effects=True, vmem_limit_bytes=64 * 1024 * 1024
        ),
    )(*arrays)
    pair_grad, proj_wgrad, gate_wgrad = pl.pallas_call(
        flush,
        out_shape=shapes,
        in_specs=[hbm] * 3,
        out_specs=(hbm, hbm, hbm),
        scratch_shapes=[pltpu.VMEM(a.shape, a.dtype) for a in shapes] + [dma((2, 3))],
        compiler_params=pltpu.CompilerParams(vmem_limit_bytes=64 * 1024 * 1024),
    )(*made)
    return pair_grad.reshape(tile, tile, width), proj_wgrad, gate_wgrad


def local(pair_norm, *rest):
    rows, cols = lax.axis_size("row"), lax.axis_size("col")
    tile_rows, tile_cols, width = pair_norm.shape
    hidden = rest[7].shape[0]
    team = rows * cols
    fits = (
        rows == cols == 4
        and tile_rows == tile_cols
        and tile_rows % 16 == 0
        and tile_rows <= 32
        and hidden == width
        and width == 128
    )
    return (fused if fits else plain)(pair_norm, *rest)


def solution(mesh):
    placed = (
        P(("groups", "row"), "col", None),
        P(("groups", "row"), "col"),
        P(("groups", "row"), "col", None),
        P(("groups", "row"), "col"),
        P(("groups", "row"), "col", None),
        P("groups"),
        P(),
        P(),
        P(),
        P(),
        P(),
    )
    return jax.shard_map(
        local,
        mesh=mesh,
        in_specs=placed,
        out_specs=(P(("groups", "row"), "col", None), P("groups", None), P("groups", None)),
        check_vma=False,
    )
```

```python
import functools

import jax
import jax.numpy as jnp
from jax import lax
from jax.experimental import pallas as pl
from jax.experimental.pallas import tpu as pltpu
from jax.sharding import PartitionSpec as P


def spread(x, axis, root):
    mine = lax.axis_index(axis) == root
    return lax.psum(jnp.where(mine, x, jnp.zeros_like(x)), axis)


def plain(
    pair_norm,
    pair_rstd,
    out_norm,
    out_rstd,
    grad_out,
    token_mask,
    proj_weight,
    gate_weight,
    out_weight,
    out_gain,
    out_bias,
):
    f32 = jnp.float32
    tile_rows, tile_cols, width = pair_norm.shape
    hidden = out_weight.shape[0]
    cells = tile_rows * tile_cols
    col_ratio = lax.axis_size("col") // lax.axis_size("row")
    row_at = lax.axis_index("row")
    col_at = lax.axis_index("col")
    mask_vals = token_mask.astype(f32)
    mask_rows = lax.dynamic_slice_in_dim(mask_vals, row_at * tile_rows, tile_rows)
    mask_cols = lax.dynamic_slice_in_dim(mask_vals, col_at * tile_cols, tile_cols)
    pair_mask = (mask_rows[:, None] * mask_cols[None, :])[:, :, None]
    flat_norm = pair_norm.reshape(cells, width)
    projected = jnp.dot(flat_norm, proj_weight, preferred_element_type=f32).reshape(
        tile_rows, tile_cols, 4 * hidden
    )
    left_gate = jax.nn.sigmoid(projected[..., :hidden])
    left_value = projected[..., hidden : 2 * hidden]
    right_gate = jax.nn.sigmoid(projected[..., 2 * hidden : 3 * hidden])
    right_value = projected[..., 3 * hidden :]
    left_proj = (pair_mask * left_gate * left_value).astype(jnp.bfloat16)
    right_proj = (pair_mask * right_gate * right_value).astype(jnp.bfloat16)
    gate_sig = jax.nn.sigmoid(jnp.dot(flat_norm, gate_weight, preferred_element_type=f32))
    hat_out = out_norm.reshape(cells, hidden).astype(f32)
    normed_out = (hat_out * out_gain + out_bias).astype(jnp.bfloat16)
    update = jnp.dot(normed_out, out_weight, preferred_element_type=f32)
    upstream = grad_out.reshape(cells, width).astype(f32)
    gate_grad = (upstream * update * gate_sig * (1.0 - gate_sig)).astype(jnp.bfloat16)
    update_grad = (upstream * gate_sig).astype(jnp.bfloat16)
    gate_part = lax.dot_general(
        flat_norm, gate_grad, (((0,), (0,)), ((), ())), preferred_element_type=f32
    )
    normed_grad = (
        lax.dot_general(
            update_grad, out_weight, (((1,), (1,)), ((), ())), preferred_element_type=f32
        )
        * out_gain
    )
    tri_grad = out_rstd.reshape(cells, 1) * (
        normed_grad
        - jnp.mean(normed_grad, axis=-1, keepdims=True)
        - hat_out * jnp.mean(normed_grad * hat_out, axis=-1, keepdims=True)
    )
    tri_grad = tri_grad.astype(jnp.bfloat16).reshape(tile_rows, tile_cols, hidden)
    left_cols, right_cols = (
        lax.all_gather(left_proj, "row", axis=0, tiled=True),
        lax.all_gather(right_proj, "row", axis=0, tiled=True),
    )
    left_total = lax.dot_general(
        lax.all_gather(tri_grad, "col", axis=1, tiled=True),
        right_cols,
        (((1,), (0,)), ((2,), (2,))),
        preferred_element_type=f32,
    )
    grad_cols = lax.all_gather(tri_grad, "row", axis=0, tiled=True)
    blocks = []
    for offset in range(col_ratio):
        panel = spread(grad_cols, "col", row_at * col_ratio + offset)
        blocks.append(
            lax.dot_general(
                panel, left_cols, (((0,), (0,)), ((2,), (2,))), preferred_element_type=f32
            )
        )
    right_turned = jnp.concatenate(blocks, axis=1)
    left_grad = jnp.transpose(left_total, (1, 2, 0))
    right_grad = jnp.transpose(right_turned, (1, 2, 0))
    proj_grad = (
        jnp.concatenate(
            [
                left_grad * pair_mask * left_value * left_gate * (1.0 - left_gate),
                left_grad * pair_mask * left_gate,
                right_grad * pair_mask * right_value * right_gate * (1.0 - right_gate),
                right_grad * pair_mask * right_gate,
            ],
            axis=-1,
        )
        .astype(jnp.bfloat16)
        .reshape(cells, 4 * hidden)
    )
    proj_part = lax.dot_general(
        flat_norm, proj_grad, (((0,), (0,)), ((), ())), preferred_element_type=f32
    )
    proj_wgrad, gate_wgrad = lax.psum((proj_part, gate_part), ("row", "col"))
    norm_grad = lax.dot_general(
        gate_grad, gate_weight, (((1,), (1,)), ((), ())), preferred_element_type=f32
    ) + lax.dot_general(
        proj_grad, proj_weight, (((1,), (1,)), ((), ())), preferred_element_type=f32
    )
    pair_vals = flat_norm.astype(f32)
    pair_grad = pair_rstd.reshape(cells, 1) * (
        norm_grad
        - jnp.mean(norm_grad, axis=-1, keepdims=True)
        - pair_vals * jnp.mean(norm_grad * pair_vals, axis=-1, keepdims=True)
    )
    return (pair_grad.reshape(tile_rows, tile_cols, width), proj_wgrad, gate_wgrad)


F32 = jnp.float32
BF16 = jnp.bfloat16
MESH = pl.DeviceIdType.MESH
ROWS_DOT = (((0,), (0,)), ((), ()))
LANES_DOT = (((1,), (1,)), ((), ()))
GROUP = 4


def kernel(
    side,
    tile,
    x_hbm,
    pair_rstd_hbm,
    hat_hbm,
    out_rstd_hbm,
    up_hbm,
    mask_hbm,
    proj_hbm,
    gate_hbm,
    out_hbm,
    gain_hbm,
    bias_hbm,
    pair_out,
    proj_out,
    gate_out,
    x_ref,
    pair_rstd_ref,
    hat_ref,
    out_rstd_ref,
    up_ref,
    mask_in,
    proj_ref,
    gate_ref,
    out_ref,
    gain_ref,
    bias_ref,
    mask_ref,
    tri_all,
    right_all,
    part_out,
    part_in,
    relay_in,
    left32,
    tri32,
    right32,
    left_acc,
    left_a,
    left_b,
    right_a,
    right_b,
    gate_grad,
    proj_grad,
    gate_acc,
    proj_acc,
    w_out,
    w_in,
    w_all,
    g_out,
    g_in,
    g_all,
    gate32,
    load_sem,
    tri_send,
    tri_recv,
    right_send,
    right_recv,
    part_send,
    part_recv,
    relay_recv,
    w_send,
    w_recv,
    all_send,
    all_recv,
):
    loads = [
        pltpu.make_async_copy(source, target, load_sem.at[k])
        for k, (source, target) in enumerate(
            (
                (x_hbm, x_ref),
                (hat_hbm, hat_ref),
                (up_hbm, up_ref),
                (gate_hbm, gate_ref),
                (out_hbm, out_ref),
                (out_rstd_hbm, out_rstd_ref),
                (gain_hbm, gain_ref),
                (bias_hbm, bias_ref),
                (mask_hbm, mask_in),
                (proj_hbm, proj_ref),
                (pair_rstd_hbm, pair_rstd_ref),
            )
        )
    ]
    for load in loads:
        load.start()

    row = lax.axis_index("row")
    col = lax.axis_index("col")
    me = row * side + col
    team = side * side
    width = x_ref.shape[-1]
    step_rows = 8
    chunks = tile // step_rows
    cells = step_rows * tile
    part = tile // 2
    sibling = row + 1 - 2 * lax.rem(row, 2)
    across = lax.rem(row + 2, side)
    beyond = lax.rem(sibling + 2, side)

    barrier = pltpu.get_barrier_semaphore()

    def place(peer):
        return {"row": peer // side, "col": lax.rem(peer, side)}

    def greet(off, carry):
        pl.semaphore_signal(
            barrier, inc=1, device_id=place(lax.rem(me + off, team)), device_id_type=MESH
        )
        return carry

    lax.fori_loop(1, team, greet, 0)

    def spot(n):
        return pl.ds(pl.multiple_of(n * cells, cells), cells)

    def lead(n):
        return pl.ds(n * step_rows, step_rows)

    def spread_cells(ref, n):
        rows = ref[pl.ds(pl.multiple_of(n * step_rows, step_rows), step_rows), :]
        return jnp.broadcast_to(rows[:, :, None], (step_rows, tile, width)).reshape(cells, width)

    def remote(source, target, send, recv, where):
        return pltpu.make_async_remote_copy(
            src_ref=source,
            dst_ref=target,
            send_sem=send,
            recv_sem=recv,
            device_id=where,
            device_id_type=MESH,
        )

    def tri_copy(slot, h, sem, peer):
        piece = tri_all.at[slot, :, pl.ds(h * part, part), :]
        return remote(piece, piece, tri_send.at[sem, h], tri_recv.at[slot, h], {"col": peer})

    def right_copy(slot, sem, peer):
        return remote(
            right_all.at[slot],
            right_all.at[slot],
            right_send.at[sem],
            right_recv.at[slot],
            {"row": peer},
        )

    def part_copy(block, h, kind, peer):
        here = pl.ds(h * part, part)
        return remote(
            part_out.at[block, here],
            part_in.at[kind, here],
            part_send.at[block, h],
            part_recv.at[kind, h],
            {"row": peer},
        )

    def relay_copy(block, h):
        here = pl.ds(h * part, part)
        return remote(
            part_out.at[block, here],
            relay_in.at[here],
            part_send.at[block, h],
            relay_recv.at[h],
            {"row": sibling},
        )

    def w_copy(k, peer, source):
        return remote(
            g_out.at[peer] if k == 2 else w_out.at[k, peer],
            g_in.at[source] if k == 2 else w_in.at[k, source],
            w_send.at[k, peer],
            w_recv.at[k, source],
            place(peer),
        )

    def all_copy(k, peer, source):
        held = g_all.at[source] if k == 2 else w_all.at[k, source]
        return remote(
            held,
            held,
            all_send.at[k, peer],
            all_recv.at[k, source],
            place(peer),
        )

    gate_acc[...] = jnp.zeros_like(gate_acc)
    proj_acc[...] = jnp.zeros_like(proj_acc)
    upper = col // 2
    inner = lax.rem(col + upper, 2)

    def mirror(t):
        return t + upper * (3 - 2 * t)

    def block_at(s):
        return mirror(s if s >= 2 else inner + s * (1 - 2 * inner))

    toward_end, toward_middle = mirror(0), mirror(inner + 1)

    for load in loads[:8]:
        load.wait()

    def first(h):
        span = pl.ds(h * part, part)

        def body(n, carry):
            rows = 2 * step_rows
            lines = pl.ds(pl.multiple_of(n * rows, rows), rows)
            gate = jax.nn.sigmoid(
                jnp.dot(
                    x_ref[lines, span, :].reshape(cells, width),
                    gate_ref[...],
                    preferred_element_type=F32,
                )
            )
            gate32[lines, span, :] = gate.reshape(rows, part, width)
            hat = hat_ref[lines, span, :].reshape(cells, width).astype(F32)
            up = up_ref[lines, span, :].reshape(cells, width).astype(F32)
            dy = (
                lax.dot_general(
                    (up * gate).astype(BF16), out_ref[...], LANES_DOT, preferred_element_type=F32
                )
                * gain_ref[...]
            )
            rstd = out_rstd_ref[lines, :][:, h * part : (h + 1) * part]
            rstd = jnp.broadcast_to(rstd[:, :, None], (rows, part, width)).reshape(cells, width)
            tri = rstd * (
                dy
                - jnp.mean(dy, axis=-1, keepdims=True)
                - hat * jnp.mean(dy * hat, axis=-1, keepdims=True)
            )
            tri_all[col, lines, span, :] = tri.astype(BF16).reshape(rows, part, width)
            return carry

        lax.fori_loop(0, tile // (2 * step_rows), body, 0)

    for h in range(2):
        first(h)
        if h == 0:
            pl.semaphore_wait(barrier, team - 1)
        tri_copy(col, h, 0, toward_middle).start()

        @pl.when(inner == 1)
        def _(h=h):
            tri_copy(col, h, 1, toward_end).start()

    for load in loads[8:]:
        load.wait()

    def forward_to(s):
        return toward_middle if s == 1 else toward_end

    def take_tri(s, h):
        block = block_at(s)
        tri_copy(block, h, 0, block).wait_recv()

        @pl.when(inner == 1)
        def _():
            tri_copy(block, h, s + 1, forward_to(s)).start()

    mask_ref[...] = jnp.transpose(
        jnp.broadcast_to(mask_in[...].astype(F32), (width, mask_in.shape[-1]))
    )
    col_mask = mask_ref[pl.ds(pl.multiple_of(col * tile, tile), tile), :]

    def second(n, carry):
        here = spot(n)
        proj = jnp.dot(x_ref[lead(n)].reshape(cells, width), proj_ref[...], preferred_element_type=F32)
        at = pl.multiple_of(row * tile + n * step_rows, step_rows)
        row_mask = mask_ref[pl.ds(at, step_rows), :]
        mask = (row_mask[:, None, :] * col_mask[None, :, :]).reshape(cells, width)
        for base, is_left in ((0, True), (2 * width, False)):
            sig = jax.nn.sigmoid(proj[:, base : base + width])
            value = proj[:, base + width : base + 2 * width]
            open_ = mask * sig
            made = (open_ * value).astype(BF16)
            slope = open_ * value * (1.0 - sig)
            if is_left:
                left32[lead(n)] = made.astype(F32).reshape(step_rows, tile, width)
                left_a[here, :] = slope
                left_b[here, :] = open_
            else:
                right_all[row, lead(n)] = made.reshape(step_rows, tile, width)
                right_a[here, :] = slope
                right_b[here, :] = open_
        return carry

    lax.fori_loop(0, chunks, second, 0)
    right_copy(row, 0, across).start()
    right_copy(row, 1, sibling).start()

    def do_part(s, h):
        block = block_at(s)
        span = pl.ds(h * part, part)
        tri32[:, span, :] = tri_all[block, :, span, :].astype(F32)

        def body(g, carry):
            at = h * part + g * GROUP
            sums = [None] * GROUP
            for i in range(tile):
                mine = left32[i]
                for q in range(GROUP):
                    term = tri32[i, pl.ds(at + q, 1), :] * mine
                    sums[q] = term if sums[q] is None else sums[q] + term
            for q in range(GROUP):
                part_out[block, at + q] = sums[q].astype(BF16)
            return carry

        lax.fori_loop(0, part // GROUP, body, 0)

        @pl.when(block == sibling)
        def _():
            part_copy(block, h, 0, sibling).start()

        @pl.when(block == beyond)
        def _():
            relay_copy(block, h).start()

    def do_relay(s, h):
        block = block_at(s)
        span = pl.ds(h * part, part)

        @pl.when(block == across)
        def _():
            relay_copy(block, h).wait_recv()
            part_out[block, span] = (
                part_out[block, span].astype(F32) + relay_in[span].astype(F32)
            ).astype(BF16)
            part_copy(block, h, 1, across).start()

    def do_left(s):
        block = block_at(s)
        right32[...] = right_all[block].astype(F32)

        def body(g, carry):
            at = g * GROUP
            sums = [None if s == 0 else left_acc[at + q] for q in range(GROUP)]
            for j in range(tile):
                mine = right32[j]
                for q in range(GROUP):
                    term = tri32[at + q, pl.ds(j, 1), :] * mine
                    sums[q] = term if sums[q] is None else sums[q] + term
            for q in range(GROUP):
                left_acc[at + q] = sums[q]
            return carry

        lax.fori_loop(0, tile // GROUP, body, 0)

    piece = 2 * width // team
    gate_piece = width // team

    def send_pieces(k):
        if k == 2:
            g_out[...] = gate_acc[...].reshape(team, gate_piece, width)
        else:
            half = proj_acc[2 * k * width : 2 * (k + 1) * width, :]
            w_out[k] = half.reshape(team, piece, width).astype(BF16)

        def body(off, carry):
            w_copy(k, lax.rem(me + off, team), me).start()
            return carry

        lax.fori_loop(1, team, body, 0)
        if k == 2:
            g_in[me] = g_out[me]
        else:
            w_in[k, me] = w_out[k, me]

    def send_totals(k):
        def body(off, carry):
            w_copy(k, me, lax.rem(me + off, team)).wait_recv()
            return carry

        lax.fori_loop(1, team, body, 0)
        parts = g_in if k == 2 else w_in.at[k]
        total = parts[0].astype(F32)
        for p in range(1, team):
            total = total + parts[p].astype(F32)
        if k == 2:
            g_all[me] = total
        else:
            w_all[k, me] = total.astype(BF16)

        def push(off, carry):
            all_copy(k, lax.rem(me + off, team), me).start()
            return carry

        lax.fori_loop(1, team, push, 0)

    for h in range(2):
        do_part(0, h)

    def third(n, carry):
        here = spot(n)
        gate = gate32[lead(n)].reshape(cells, width)
        hat = hat_ref[lead(n)].reshape(cells, width).astype(F32)
        y = (hat * gain_ref[...] + bias_ref[...]).astype(BF16)
        update = jnp.dot(y, out_ref[...], preferred_element_type=F32)
        up = up_ref[lead(n)].reshape(cells, width).astype(F32)
        gate_grad[here, :] = (up * update * gate * (1.0 - gate)).astype(BF16)
        gate_acc[...] += lax.dot_general(
            x_ref[lead(n)].reshape(cells, width), gate_grad[here, :], ROWS_DOT, preferred_element_type=F32
        )
        return carry

    lax.fori_loop(0, chunks, third, 0)
    for h in range(2):
        do_relay(0, h)
    for h in range(2):
        take_tri(1, h)
    right_copy(across, 0, across).wait_recv()
    right_copy(across, 2, sibling).start()
    right_copy(sibling, 0, sibling).wait_recv()
    right_copy(beyond, 0, sibling).wait_recv()
    do_left(0)
    for s in range(1, side):
        for h in range(2):
            if s > 1:
                take_tri(s, h)
            do_part(s, h)
        if s < side - 1:
            do_left(s)
        for h in range(2):
            do_relay(s, h)
        if s == side - 1:
            send_pieces(2)
            do_left(s)

    def weights(n, grads, base):
        here = spot(n)
        x = x_ref[lead(n)].reshape(cells, width)
        for q, grad in enumerate(grads):
            grad = grad.astype(BF16)
            at = (base + q) * width
            proj_grad[here, at : at + width] = grad
            proj_acc[at : at + width, :] += lax.dot_general(
                x, grad, ROWS_DOT, preferred_element_type=F32
            )

    def left_weights(n, carry):
        here = spot(n)
        grad = left_acc[lead(n)].reshape(cells, width)
        weights(n, (grad * left_a[here, :], grad * left_b[here, :]), 0)
        return carry

    def right_weights(n, carry):
        here = spot(n)
        grad = part_out[row, lead(n)].astype(F32)
        for kind in range(2):
            grad = grad + part_in[kind, lead(n)].astype(F32)
        grad = grad.reshape(cells, width)
        weights(n, (grad * right_a[here, :], grad * right_b[here, :]), 2)
        return carry

    lax.fori_loop(0, chunks, left_weights, 0)
    send_pieces(0)
    send_totals(2)
    for kind in range(2):
        for h in range(2):
            part_copy(row, h, kind, sibling).wait_recv()
    lax.fori_loop(0, chunks, right_weights, 0)
    send_pieces(1)
    send_totals(0)

    def last(n, carry):
        here = spot(n)
        grad = lax.dot_general(
            gate_grad[here, :], gate_ref[...], LANES_DOT, preferred_element_type=F32
        ) + lax.dot_general(
            proj_grad[here, :], proj_ref[...], LANES_DOT, preferred_element_type=F32
        )
        x = x_ref[lead(n)].reshape(cells, width).astype(F32)
        pair_out[here, :] = spread_cells(pair_rstd_ref, n) * (
            grad
            - jnp.mean(grad, axis=-1, keepdims=True)
            - x * jnp.mean(grad * x, axis=-1, keepdims=True)
        )
        return carry

    lax.fori_loop(0, chunks // 2, last, 0)
    send_totals(1)
    lax.fori_loop(chunks // 2, chunks, last, 0)

    for h in range(2):
        tri_copy(col, h, 0, toward_middle).wait_send()

        @pl.when(inner == 1)
        def _(h=h):
            tri_copy(col, h, 1, toward_end).wait_send()
            for s in range(1, side):
                tri_copy(block_at(s), h, s + 1, forward_to(s)).wait_send()

        part_copy(sibling, h, 0, sibling).wait_send()
        relay_copy(beyond, h).wait_send()
        part_copy(across, h, 1, across).wait_send()
    right_copy(row, 0, across).wait_send()
    right_copy(row, 1, sibling).wait_send()
    right_copy(across, 2, sibling).wait_send()

    def finish(off, carry):
        peer = lax.rem(me + off, team)
        for k in range(3):
            w_copy(k, peer, me).wait_send()
        return carry

    lax.fori_loop(1, team, finish, 0)

    def get_totals(off, carry):
        peer = lax.rem(me + off, team)
        for k in range(3):
            all_copy(k, me, peer).wait_recv()
        return carry

    lax.fori_loop(1, team, get_totals, 0)

    def finish_totals(off, carry):
        peer = lax.rem(me + off, team)
        for k in range(3):
            all_copy(k, peer, me).wait_send()
        return carry

    lax.fori_loop(1, team, finish_totals, 0)

    each = width // piece
    for q in range(4):
        k, at = q // 2, (q % 2) * each
        proj_out[:, q * width : (q + 1) * width] = (
            w_all[k, at : at + each].astype(F32).reshape(width, width)
        )
    gate_out[...] = g_all[...].reshape(width, width)


def flush(*refs):
    count = len(refs) // 3
    sources, targets, held = refs[:count], refs[count : 2 * count], refs[2 * count : -1]
    sem = refs[-1]
    reads = [
        pltpu.make_async_copy(sources[k], held[k], sem.at[0, k]) for k in range(count)
    ]
    writes = [
        pltpu.make_async_copy(held[k], targets[k], sem.at[1, k]) for k in range(count)
    ]
    for read in reads:
        read.start()
    for read, write in zip(reads, writes):
        read.wait()
        write.start()
    for write in writes:
        write.wait()


def fused(
    pair_norm,
    pair_rstd,
    out_norm,
    out_rstd,
    grad_out,
    token_mask,
    proj_weight,
    gate_weight,
    out_weight,
    out_gain,
    out_bias,
):
    tile, _, width = pair_norm.shape
    side = lax.axis_size("row")
    team = side * side
    cells = tile * tile
    piece = 2 * width // team
    tokens = token_mask.shape[0]
    vmem = pl.BlockSpec(memory_space=pltpu.VMEM)
    hbm = pl.BlockSpec(memory_space=pltpu.HBM)
    dma = pltpu.SemaphoreType.DMA
    shapes = (
        jax.ShapeDtypeStruct((cells, width), F32),
        jax.ShapeDtypeStruct((width, 4 * width), F32),
        jax.ShapeDtypeStruct((width, width), F32),
    )
    arrays = (
        pair_norm,
        pair_rstd,
        out_norm,
        out_rstd,
        grad_out,
        token_mask.reshape(1, tokens),
        proj_weight,
        gate_weight,
        out_weight,
        out_gain.reshape(1, width),
        out_bias.reshape(1, width),
    )
    made = pl.pallas_call(
        functools.partial(kernel, side, tile),
        out_shape=shapes,
        in_specs=[hbm] * 11,
        out_specs=(vmem, vmem, vmem),
        scratch_shapes=[pltpu.VMEM(a.shape, a.dtype) for a in arrays]
        + [
            pltpu.VMEM((tokens, width), F32),
            pltpu.VMEM((side, tile, tile, width), BF16),
            pltpu.VMEM((side, tile, tile, width), BF16),
            pltpu.VMEM((side, tile, tile, width), BF16),
            pltpu.VMEM((2, tile, tile, width), BF16),
            pltpu.VMEM((tile, tile, width), BF16),
            pltpu.VMEM((tile, tile, width), F32),
            pltpu.VMEM((tile, tile, width), F32),
            pltpu.VMEM((tile, tile, width), F32),
            pltpu.VMEM((tile, tile, width), F32),
            pltpu.VMEM((cells, width), F32),
            pltpu.VMEM((cells, width), F32),
            pltpu.VMEM((cells, width), F32),
            pltpu.VMEM((cells, width), F32),
            pltpu.VMEM((cells, width), BF16),
            pltpu.VMEM((cells, 4 * width), BF16),
            pltpu.VMEM((width, width), F32),
            pltpu.VMEM((4 * width, width), F32),
            pltpu.VMEM((2, team, piece, width), BF16),
            pltpu.VMEM((2, team, piece, width), BF16),
            pltpu.VMEM((2, team, piece, width), BF16),
            pltpu.VMEM((team, width // team, width), F32),
            pltpu.VMEM((team, width // team, width), F32),
            pltpu.VMEM((team, width // team, width), F32),
            pltpu.VMEM((tile, tile, width), F32),
            dma((11,)),
            dma((side + 1, 2)),
            dma((side, 2)),
            dma((side,)),
            dma((side,)),
            dma((side, 2)),
            dma((2, 2)),
            dma((2,)),
            dma((3, team)),
            dma((3, team)),
            dma((3, team)),
            dma((3, team)),
        ],
        compiler_params=pltpu.CompilerParams(
            collective_id=0, has_side_effects=True, vmem_limit_bytes=64 * 1024 * 1024
        ),
    )(*arrays)
    pair_grad, proj_wgrad, gate_wgrad = pl.pallas_call(
        flush,
        out_shape=shapes,
        in_specs=[hbm] * 3,
        out_specs=(hbm, hbm, hbm),
        scratch_shapes=[pltpu.VMEM(a.shape, a.dtype) for a in shapes] + [dma((2, 3))],
        compiler_params=pltpu.CompilerParams(vmem_limit_bytes=64 * 1024 * 1024),
    )(*made)
    return pair_grad.reshape(tile, tile, width), proj_wgrad, gate_wgrad


def local(pair_norm, *rest):
    rows, cols = lax.axis_size("row"), lax.axis_size("col")
    tile_rows, tile_cols, width = pair_norm.shape
    hidden = rest[7].shape[0]
    team = rows * cols
    fits = (
        rows == cols == 4
        and tile_rows == tile_cols
        and tile_rows % 16 == 0
        and tile_rows <= 32
        and hidden == width
        and width == 128
    )
    return (fused if fits else plain)(pair_norm, *rest)


def solution(mesh):
    placed = (
        P(("groups", "row"), "col", None),
        P(("groups", "row"), "col"),
        P(("groups", "row"), "col", None),
        P(("groups", "row"), "col"),
        P(("groups", "row"), "col", None),
        P("groups"),
        P(),
        P(),
        P(),
        P(),
        P(),
    )
    return jax.shard_map(
        local,
        mesh=mesh,
        in_specs=placed,
        out_specs=(P(("groups", "row"), "col", None), P("groups", None), P("groups", None)),
        check_vma=False,
    )
```

```python
import functools

import jax
import jax.numpy as jnp
from jax import lax
from jax.experimental import pallas as pl
from jax.experimental.pallas import tpu as pltpu
from jax.sharding import PartitionSpec as P


def spread(x, axis, root):
    mine = lax.axis_index(axis) == root
    return lax.psum(jnp.where(mine, x, jnp.zeros_like(x)), axis)


def plain(
    pair_norm,
    pair_rstd,
    out_norm,
    out_rstd,
    grad_out,
    token_mask,
    proj_weight,
    gate_weight,
    out_weight,
    out_gain,
    out_bias,
):
    f32 = jnp.float32
    tile_rows, tile_cols, width = pair_norm.shape
    hidden = out_weight.shape[0]
    cells = tile_rows * tile_cols
    col_ratio = lax.axis_size("col") // lax.axis_size("row")
    row_at = lax.axis_index("row")
    col_at = lax.axis_index("col")
    mask_vals = token_mask.astype(f32)
    mask_rows = lax.dynamic_slice_in_dim(mask_vals, row_at * tile_rows, tile_rows)
    mask_cols = lax.dynamic_slice_in_dim(mask_vals, col_at * tile_cols, tile_cols)
    pair_mask = (mask_rows[:, None] * mask_cols[None, :])[:, :, None]
    flat_norm = pair_norm.reshape(cells, width)
    projected = jnp.dot(flat_norm, proj_weight, preferred_element_type=f32).reshape(
        tile_rows, tile_cols, 4 * hidden
    )
    left_gate = jax.nn.sigmoid(projected[..., :hidden])
    left_value = projected[..., hidden : 2 * hidden]
    right_gate = jax.nn.sigmoid(projected[..., 2 * hidden : 3 * hidden])
    right_value = projected[..., 3 * hidden :]
    left_proj = (pair_mask * left_gate * left_value).astype(jnp.bfloat16)
    right_proj = (pair_mask * right_gate * right_value).astype(jnp.bfloat16)
    gate_sig = jax.nn.sigmoid(jnp.dot(flat_norm, gate_weight, preferred_element_type=f32))
    hat_out = out_norm.reshape(cells, hidden).astype(f32)
    normed_out = (hat_out * out_gain + out_bias).astype(jnp.bfloat16)
    update = jnp.dot(normed_out, out_weight, preferred_element_type=f32)
    upstream = grad_out.reshape(cells, width).astype(f32)
    gate_grad = (upstream * update * gate_sig * (1.0 - gate_sig)).astype(jnp.bfloat16)
    update_grad = (upstream * gate_sig).astype(jnp.bfloat16)
    gate_part = lax.dot_general(
        flat_norm, gate_grad, (((0,), (0,)), ((), ())), preferred_element_type=f32
    )
    normed_grad = (
        lax.dot_general(
            update_grad, out_weight, (((1,), (1,)), ((), ())), preferred_element_type=f32
        )
        * out_gain
    )
    tri_grad = out_rstd.reshape(cells, 1) * (
        normed_grad
        - jnp.mean(normed_grad, axis=-1, keepdims=True)
        - hat_out * jnp.mean(normed_grad * hat_out, axis=-1, keepdims=True)
    )
    tri_grad = tri_grad.astype(jnp.bfloat16).reshape(tile_rows, tile_cols, hidden)
    left_cols, right_cols = (
        lax.all_gather(left_proj, "row", axis=0, tiled=True),
        lax.all_gather(right_proj, "row", axis=0, tiled=True),
    )
    left_total = lax.dot_general(
        lax.all_gather(tri_grad, "col", axis=1, tiled=True),
        right_cols,
        (((1,), (0,)), ((2,), (2,))),
        preferred_element_type=f32,
    )
    grad_cols = lax.all_gather(tri_grad, "row", axis=0, tiled=True)
    blocks = []
    for offset in range(col_ratio):
        panel = spread(grad_cols, "col", row_at * col_ratio + offset)
        blocks.append(
            lax.dot_general(
                panel, left_cols, (((0,), (0,)), ((2,), (2,))), preferred_element_type=f32
            )
        )
    right_turned = jnp.concatenate(blocks, axis=1)
    left_grad = jnp.transpose(left_total, (1, 2, 0))
    right_grad = jnp.transpose(right_turned, (1, 2, 0))
    proj_grad = (
        jnp.concatenate(
            [
                left_grad * pair_mask * left_value * left_gate * (1.0 - left_gate),
                left_grad * pair_mask * left_gate,
                right_grad * pair_mask * right_value * right_gate * (1.0 - right_gate),
                right_grad * pair_mask * right_gate,
            ],
            axis=-1,
        )
        .astype(jnp.bfloat16)
        .reshape(cells, 4 * hidden)
    )
    proj_part = lax.dot_general(
        flat_norm, proj_grad, (((0,), (0,)), ((), ())), preferred_element_type=f32
    )
    proj_wgrad, gate_wgrad = lax.psum((proj_part, gate_part), ("row", "col"))
    norm_grad = lax.dot_general(
        gate_grad, gate_weight, (((1,), (1,)), ((), ())), preferred_element_type=f32
    ) + lax.dot_general(
        proj_grad, proj_weight, (((1,), (1,)), ((), ())), preferred_element_type=f32
    )
    pair_vals = flat_norm.astype(f32)
    pair_grad = pair_rstd.reshape(cells, 1) * (
        norm_grad
        - jnp.mean(norm_grad, axis=-1, keepdims=True)
        - pair_vals * jnp.mean(norm_grad * pair_vals, axis=-1, keepdims=True)
    )
    return (pair_grad.reshape(tile_rows, tile_cols, width), proj_wgrad, gate_wgrad)


F32 = jnp.float32
BF16 = jnp.bfloat16
MESH = pl.DeviceIdType.MESH
ROWS_DOT = (((0,), (0,)), ((), ()))
LANES_DOT = (((1,), (1,)), ((), ()))
GROUP = 4


def kernel(
    side,
    tile,
    x_hbm,
    pair_rstd_hbm,
    hat_hbm,
    out_rstd_hbm,
    up_hbm,
    mask_hbm,
    proj_hbm,
    gate_hbm,
    out_hbm,
    gain_hbm,
    bias_hbm,
    pair_out,
    proj_out,
    gate_out,
    x_ref,
    pair_rstd_ref,
    hat_ref,
    out_rstd_ref,
    up_ref,
    mask_in,
    proj_ref,
    gate_ref,
    out_ref,
    gain_ref,
    bias_ref,
    mask_ref,
    tri_all,
    right_all,
    part_out,
    part_in,
    relay_in,
    left32,
    tri32,
    right32,
    left_acc,
    left_a,
    left_b,
    right_a,
    right_b,
    gate_grad,
    proj_grad,
    gate_acc,
    proj_acc,
    w_out,
    w_in,
    c_all,
    w_all,
    g_out,
    g_in,
    g_all,
    gate32,
    load_sem,
    tri_send,
    tri_recv,
    right_send,
    right_recv,
    part_send,
    part_recv,
    relay_recv,
    w_send,
    w_recv,
    all_send,
    all_recv,
):
    loads = [
        pltpu.make_async_copy(source, target, load_sem.at[k])
        for k, (source, target) in enumerate(
            (
                (x_hbm, x_ref),
                (hat_hbm, hat_ref),
                (up_hbm, up_ref),
                (gate_hbm, gate_ref),
                (out_hbm, out_ref),
                (out_rstd_hbm, out_rstd_ref),
                (gain_hbm, gain_ref),
                (bias_hbm, bias_ref),
                (mask_hbm, mask_in),
                (proj_hbm, proj_ref),
                (pair_rstd_hbm, pair_rstd_ref),
            )
        )
    ]
    for load in loads:
        load.start()

    row = lax.axis_index("row")
    col = lax.axis_index("col")
    me = row * side + col
    team = side * side
    width = x_ref.shape[-1]
    step_rows = 8
    chunks = tile // step_rows
    cells = step_rows * tile
    part = tile // 2
    sibling = row + 1 - 2 * lax.rem(row, 2)
    across = lax.rem(row + 2, side)
    beyond = lax.rem(sibling + 2, side)

    barrier = pltpu.get_barrier_semaphore()

    def place(peer):
        return {"row": peer // side, "col": lax.rem(peer, side)}

    def greet(off, carry):
        pl.semaphore_signal(
            barrier, inc=1, device_id=place(lax.rem(me + off, team)), device_id_type=MESH
        )
        return carry

    lax.fori_loop(1, team, greet, 0)

    def spot(n):
        return pl.ds(pl.multiple_of(n * cells, cells), cells)

    def lead(n):
        return pl.ds(n * step_rows, step_rows)

    def spread_cells(ref, n):
        rows = ref[pl.ds(pl.multiple_of(n * step_rows, step_rows), step_rows), :]
        return jnp.broadcast_to(rows[:, :, None], (step_rows, tile, width)).reshape(cells, width)

    def remote(source, target, send, recv, where):
        return pltpu.make_async_remote_copy(
            src_ref=source,
            dst_ref=target,
            send_sem=send,
            recv_sem=recv,
            device_id=where,
            device_id_type=MESH,
        )

    def tri_copy(slot, h, sem, peer):
        piece = tri_all.at[slot, :, pl.ds(h * part, part), :]
        return remote(piece, piece, tri_send.at[sem, h], tri_recv.at[slot, h], {"col": peer})

    def right_copy(slot, sem, peer):
        return remote(
            right_all.at[slot],
            right_all.at[slot],
            right_send.at[sem],
            right_recv.at[slot],
            {"row": peer},
        )

    def part_copy(block, h, kind, peer):
        here = pl.ds(h * part, part)
        return remote(
            part_out.at[block, here],
            part_in.at[kind, here],
            part_send.at[block, h],
            part_recv.at[kind, h],
            {"row": peer},
        )

    def relay_copy(block, h):
        here = pl.ds(h * part, part)
        return remote(
            part_out.at[block, here],
            relay_in.at[here],
            part_send.at[block, h],
            relay_recv.at[h],
            {"row": sibling},
        )

    def w_copy(k, peer, source):
        return remote(
            g_out.at[peer] if k == 2 else w_out.at[k, peer],
            g_in.at[source] if k == 2 else w_in.at[k, source],
            w_send.at[k, peer],
            w_recv.at[k, source],
            place(peer),
        )

    def all_copy(k, peer, source):
        held = g_all.at[source] if k == 2 else w_all.at[k, source]
        return remote(
            held,
            held,
            all_send.at[k, peer],
            all_recv.at[k, source],
            place(peer),
        )

    gate_acc[...] = jnp.zeros_like(gate_acc)
    proj_acc[...] = jnp.zeros_like(proj_acc)
    upper = col // 2
    inner = lax.rem(col + upper, 2)

    def mirror(t):
        return t + upper * (3 - 2 * t)

    def block_at(s):
        return mirror(s if s >= 2 else inner + s * (1 - 2 * inner))

    toward_end, toward_middle = mirror(0), mirror(inner + 1)

    for load in loads[:8]:
        load.wait()

    def first(h):
        span = pl.ds(h * part, part)

        def body(n, carry):
            rows = 2 * step_rows
            lines = pl.ds(pl.multiple_of(n * rows, rows), rows)
            gate = jax.nn.sigmoid(
                jnp.dot(
                    x_ref[lines, span, :].reshape(cells, width),
                    gate_ref[...],
                    preferred_element_type=F32,
                )
            )
            gate32[lines, span, :] = gate.reshape(rows, part, width)
            hat = hat_ref[lines, span, :].reshape(cells, width).astype(F32)
            up = up_ref[lines, span, :].reshape(cells, width).astype(F32)
            dy = (
                lax.dot_general(
                    (up * gate).astype(BF16), out_ref[...], LANES_DOT, preferred_element_type=F32
                )
                * gain_ref[...]
            )
            rstd = out_rstd_ref[lines, :][:, h * part : (h + 1) * part]
            rstd = jnp.broadcast_to(rstd[:, :, None], (rows, part, width)).reshape(cells, width)
            tri = rstd * (
                dy
                - jnp.mean(dy, axis=-1, keepdims=True)
                - hat * jnp.mean(dy * hat, axis=-1, keepdims=True)
            )
            tri_all[col, lines, span, :] = tri.astype(BF16).reshape(rows, part, width)
            return carry

        lax.fori_loop(0, tile // (2 * step_rows), body, 0)

    for h in range(2):
        first(h)
        if h == 0:
            pl.semaphore_wait(barrier, team - 1)
        tri_copy(col, h, 0, toward_middle).start()

        @pl.when(inner == 1)
        def _(h=h):
            tri_copy(col, h, 1, toward_end).start()

    for load in loads[8:]:
        load.wait()

    def forward_to(s):
        return toward_middle if s == 1 else toward_end

    def take_tri(s, h):
        block = block_at(s)
        tri_copy(block, h, 0, block).wait_recv()

        @pl.when(inner == 1)
        def _():
            tri_copy(block, h, s + 1, forward_to(s)).start()

    mask_ref[...] = jnp.transpose(
        jnp.broadcast_to(mask_in[...].astype(F32), (width, mask_in.shape[-1]))
    )
    col_mask = mask_ref[pl.ds(pl.multiple_of(col * tile, tile), tile), :]

    def second(n, carry):
        here = spot(n)
        proj = jnp.dot(x_ref[lead(n)].reshape(cells, width), proj_ref[...], preferred_element_type=F32)
        at = pl.multiple_of(row * tile + n * step_rows, step_rows)
        row_mask = mask_ref[pl.ds(at, step_rows), :]
        mask = (row_mask[:, None, :] * col_mask[None, :, :]).reshape(cells, width)
        for base, is_left in ((0, True), (2 * width, False)):
            sig = jax.nn.sigmoid(proj[:, base : base + width])
            value = proj[:, base + width : base + 2 * width]
            open_ = mask * sig
            made = (open_ * value).astype(BF16)
            slope = open_ * value * (1.0 - sig)
            if is_left:
                left32[lead(n)] = made.astype(F32).reshape(step_rows, tile, width)
                left_a[here, :] = slope
                left_b[here, :] = open_
            else:
                right_all[row, lead(n)] = made.reshape(step_rows, tile, width)
                right_a[here, :] = slope
                right_b[here, :] = open_
        return carry

    lax.fori_loop(0, chunks, second, 0)
    right_copy(row, 0, across).start()
    right_copy(row, 1, sibling).start()

    def do_part(s, h):
        block = block_at(s)
        span = pl.ds(h * part, part)
        tri32[:, span, :] = tri_all[block, :, span, :].astype(F32)

        def body(g, carry):
            at = h * part + g * GROUP
            sums = [None] * GROUP
            for i in range(tile):
                mine = left32[i]
                for q in range(GROUP):
                    term = tri32[i, pl.ds(at + q, 1), :] * mine
                    sums[q] = term if sums[q] is None else sums[q] + term
            for q in range(GROUP):
                part_out[block, at + q] = sums[q].astype(BF16)
            return carry

        lax.fori_loop(0, part // GROUP, body, 0)

        @pl.when(block == sibling)
        def _():
            part_copy(block, h, 0, sibling).start()

        @pl.when(block == beyond)
        def _():
            relay_copy(block, h).start()

    def do_relay(s, h):
        block = block_at(s)
        span = pl.ds(h * part, part)

        @pl.when(block == across)
        def _():
            relay_copy(block, h).wait_recv()
            part_out[block, span] = (
                part_out[block, span].astype(F32) + relay_in[span].astype(F32)
            ).astype(BF16)
            part_copy(block, h, 1, across).start()

    def do_left(s):
        block = block_at(s)
        right32[...] = right_all[block].astype(F32)

        def body(g, carry):
            at = g * GROUP
            sums = [None if s == 0 else left_acc[at + q] for q in range(GROUP)]
            for j in range(tile):
                mine = right32[j]
                for q in range(GROUP):
                    term = tri32[at + q, pl.ds(j, 1), :] * mine
                    sums[q] = term if sums[q] is None else sums[q] + term
            for q in range(GROUP):
                left_acc[at + q] = sums[q]
            return carry

        lax.fori_loop(0, tile // GROUP, body, 0)

    piece = 2 * width // team
    gate_piece = width // team

    def quarter_copy(q, source):
        return remote(
            w_out.at[q], w_in.at[source], w_send.at[0, q], w_recv.at[0, source], {"row": q}
        )

    def col_copy(peer, source):
        held = c_all.at[source]
        return remote(held, held, w_send.at[1, peer], w_recv.at[1, source], {"col": peer})

    def row_copy(peer, source):
        held = w_all.at[source]
        return remote(held, held, all_send.at[0, peer], all_recv.at[0, source], {"row": peer})

    def send_quarters(start):
        for q in range(start, start + 2):
            w_out[q] = proj_acc[q * width : (q + 1) * width, :].astype(BF16)

            @pl.when(row != q)
            def _(q=q):
                quarter_copy(q, row).start()

            @pl.when(row == q)
            def _(q=q):
                w_in[row] = w_out[q]

    def send_pieces(k):
        if k == 2:
            g_out[...] = gate_acc[...].reshape(team, gate_piece, width)
        else:
            half = proj_acc[2 * k * width : 2 * (k + 1) * width, :]
            w_out[k] = half.reshape(team, piece, width).astype(BF16)

        def body(off, carry):
            w_copy(k, lax.rem(me + off, team), me).start()
            return carry

        lax.fori_loop(1, team, body, 0)
        if k == 2:
            g_in[me] = g_out[me]
        else:
            w_in[k, me] = w_out[k, me]

    def send_totals(k):
        def body(off, carry):
            w_copy(k, me, lax.rem(me + off, team)).wait_recv()
            return carry

        lax.fori_loop(1, team, body, 0)
        parts = g_in if k == 2 else w_in.at[k]
        total = parts[0].astype(F32)
        for p in range(1, team):
            total = total + parts[p].astype(F32)
        if k == 2:
            g_all[me] = total
        else:
            w_all[k, me] = total.astype(BF16)

        def push(off, carry):
            all_copy(k, lax.rem(me + off, team), me).start()
            return carry

        lax.fori_loop(1, team, push, 0)

    for h in range(2):
        do_part(0, h)

    def third(n, carry):
        here = spot(n)
        gate = gate32[lead(n)].reshape(cells, width)
        hat = hat_ref[lead(n)].reshape(cells, width).astype(F32)
        y = (hat * gain_ref[...] + bias_ref[...]).astype(BF16)
        update = jnp.dot(y, out_ref[...], preferred_element_type=F32)
        up = up_ref[lead(n)].reshape(cells, width).astype(F32)
        gate_grad[here, :] = (up * update * gate * (1.0 - gate)).astype(BF16)
        gate_acc[...] += lax.dot_general(
            x_ref[lead(n)].reshape(cells, width), gate_grad[here, :], ROWS_DOT, preferred_element_type=F32
        )
        return carry

    lax.fori_loop(0, chunks, third, 0)
    for h in range(2):
        do_relay(0, h)
    for h in range(2):
        take_tri(1, h)
    right_copy(across, 0, across).wait_recv()
    right_copy(across, 2, sibling).start()
    right_copy(sibling, 0, sibling).wait_recv()
    right_copy(beyond, 0, sibling).wait_recv()
    do_left(0)
    for s in range(1, side):
        for h in range(2):
            if s > 1:
                take_tri(s, h)
            do_part(s, h)
        if s < side - 1:
            do_left(s)
        for h in range(2):
            do_relay(s, h)
        if s == side - 1:
            send_pieces(2)
            do_left(s)

    def weights(n, grads, base):
        here = spot(n)
        x = x_ref[lead(n)].reshape(cells, width)
        for q, grad in enumerate(grads):
            grad = grad.astype(BF16)
            at = (base + q) * width
            proj_grad[here, at : at + width] = grad
            proj_acc[at : at + width, :] += lax.dot_general(
                x, grad, ROWS_DOT, preferred_element_type=F32
            )

    def left_weights(n, carry):
        here = spot(n)
        grad = left_acc[lead(n)].reshape(cells, width)
        weights(n, (grad * left_a[here, :], grad * left_b[here, :]), 0)
        return carry

    def right_weights(n, carry):
        here = spot(n)
        grad = part_out[row, lead(n)].astype(F32)
        for kind in range(2):
            grad = grad + part_in[kind, lead(n)].astype(F32)
        grad = grad.reshape(cells, width)
        weights(n, (grad * right_a[here, :], grad * right_b[here, :]), 2)
        return carry

    lax.fori_loop(0, chunks, left_weights, 0)
    send_quarters(0)
    send_totals(2)
    for kind in range(2):
        for h in range(2):
            part_copy(row, h, kind, sibling).wait_recv()
    lax.fori_loop(0, chunks, right_weights, 0)
    send_quarters(2)

    def last(n, carry):
        here = spot(n)
        grad = lax.dot_general(
            gate_grad[here, :], gate_ref[...], LANES_DOT, preferred_element_type=F32
        ) + lax.dot_general(
            proj_grad[here, :], proj_ref[...], LANES_DOT, preferred_element_type=F32
        )
        x = x_ref[lead(n)].reshape(cells, width).astype(F32)
        pair_out[here, :] = spread_cells(pair_rstd_ref, n) * (
            grad
            - jnp.mean(grad, axis=-1, keepdims=True)
            - x * jnp.mean(grad * x, axis=-1, keepdims=True)
        )
        return carry

    lax.fori_loop(0, 1, last, 0)
    for r in range(1, side):
        quarter_copy(row, lax.rem(row + r, side)).wait_recv()
    total = w_in[0].astype(F32)
    for r in range(1, side):
        total = total + w_in[r].astype(F32)
    c_all[col] = total.astype(BF16)
    for r in range(1, side):
        col_copy(lax.rem(col + r, side), col).start()
    lax.fori_loop(1, 3, last, 0)
    for r in range(1, side):
        col_copy(col, lax.rem(col + r, side)).wait_recv()
    total = c_all[0].astype(F32)
    for r in range(1, side):
        total = total + c_all[r].astype(F32)
    w_all[row] = total.astype(BF16)
    for r in range(1, side):
        row_copy(lax.rem(row + r, side), row).start()
    lax.fori_loop(3, chunks, last, 0)
    for r in range(1, side):
        quarter_copy(lax.rem(row + r, side), row).wait_send()
        col_copy(lax.rem(col + r, side), col).wait_send()
        row_copy(lax.rem(row + r, side), row).wait_send()
        row_copy(row, lax.rem(row + r, side)).wait_recv()

    for h in range(2):
        tri_copy(col, h, 0, toward_middle).wait_send()

        @pl.when(inner == 1)
        def _(h=h):
            tri_copy(col, h, 1, toward_end).wait_send()
            for s in range(1, side):
                tri_copy(block_at(s), h, s + 1, forward_to(s)).wait_send()

        part_copy(sibling, h, 0, sibling).wait_send()
        relay_copy(beyond, h).wait_send()
        part_copy(across, h, 1, across).wait_send()
    right_copy(row, 0, across).wait_send()
    right_copy(row, 1, sibling).wait_send()
    right_copy(across, 2, sibling).wait_send()

    def finish(off, carry):
        peer = lax.rem(me + off, team)
        for k in range(2, 3):
            w_copy(k, peer, me).wait_send()
        return carry

    lax.fori_loop(1, team, finish, 0)

    def get_totals(off, carry):
        peer = lax.rem(me + off, team)
        for k in range(2, 3):
            all_copy(k, me, peer).wait_recv()
        return carry

    lax.fori_loop(1, team, get_totals, 0)

    def finish_totals(off, carry):
        peer = lax.rem(me + off, team)
        for k in range(2, 3):
            all_copy(k, peer, me).wait_send()
        return carry

    lax.fori_loop(1, team, finish_totals, 0)

    for q in range(4):
        proj_out[:, q * width : (q + 1) * width] = w_all[q].astype(F32)
    gate_out[...] = g_all[...].reshape(width, width)


def flush(*refs):
    count = len(refs) // 3
    sources, targets, held = refs[:count], refs[count : 2 * count], refs[2 * count : -1]
    sem = refs[-1]
    reads = [
        pltpu.make_async_copy(sources[k], held[k], sem.at[0, k]) for k in range(count)
    ]
    writes = [
        pltpu.make_async_copy(held[k], targets[k], sem.at[1, k]) for k in range(count)
    ]
    for read in reads:
        read.start()
    for read, write in zip(reads, writes):
        read.wait()
        write.start()
    for write in writes:
        write.wait()


def fused(
    pair_norm,
    pair_rstd,
    out_norm,
    out_rstd,
    grad_out,
    token_mask,
    proj_weight,
    gate_weight,
    out_weight,
    out_gain,
    out_bias,
):
    tile, _, width = pair_norm.shape
    side = lax.axis_size("row")
    team = side * side
    cells = tile * tile
    piece = 2 * width // team
    tokens = token_mask.shape[0]
    vmem = pl.BlockSpec(memory_space=pltpu.VMEM)
    hbm = pl.BlockSpec(memory_space=pltpu.HBM)
    dma = pltpu.SemaphoreType.DMA
    shapes = (
        jax.ShapeDtypeStruct((cells, width), F32),
        jax.ShapeDtypeStruct((width, 4 * width), F32),
        jax.ShapeDtypeStruct((width, width), F32),
    )
    arrays = (
        pair_norm,
        pair_rstd,
        out_norm,
        out_rstd,
        grad_out,
        token_mask.reshape(1, tokens),
        proj_weight,
        gate_weight,
        out_weight,
        out_gain.reshape(1, width),
        out_bias.reshape(1, width),
    )
    made = pl.pallas_call(
        functools.partial(kernel, side, tile),
        out_shape=shapes,
        in_specs=[hbm] * 11,
        out_specs=(vmem, vmem, vmem),
        scratch_shapes=[pltpu.VMEM(a.shape, a.dtype) for a in arrays]
        + [
            pltpu.VMEM((tokens, width), F32),
            pltpu.VMEM((side, tile, tile, width), BF16),
            pltpu.VMEM((side, tile, tile, width), BF16),
            pltpu.VMEM((side, tile, tile, width), BF16),
            pltpu.VMEM((2, tile, tile, width), BF16),
            pltpu.VMEM((tile, tile, width), BF16),
            pltpu.VMEM((tile, tile, width), F32),
            pltpu.VMEM((tile, tile, width), F32),
            pltpu.VMEM((tile, tile, width), F32),
            pltpu.VMEM((tile, tile, width), F32),
            pltpu.VMEM((cells, width), F32),
            pltpu.VMEM((cells, width), F32),
            pltpu.VMEM((cells, width), F32),
            pltpu.VMEM((cells, width), F32),
            pltpu.VMEM((cells, width), BF16),
            pltpu.VMEM((cells, 4 * width), BF16),
            pltpu.VMEM((width, width), F32),
            pltpu.VMEM((4 * width, width), F32),
            pltpu.VMEM((4, width, width), BF16),
            pltpu.VMEM((4, width, width), BF16),
            pltpu.VMEM((4, width, width), BF16),
            pltpu.VMEM((4, width, width), BF16),
            pltpu.VMEM((team, width // team, width), F32),
            pltpu.VMEM((team, width // team, width), F32),
            pltpu.VMEM((team, width // team, width), F32),
            pltpu.VMEM((tile, tile, width), F32),
            dma((11,)),
            dma((side + 1, 2)),
            dma((side, 2)),
            dma((side,)),
            dma((side,)),
            dma((side, 2)),
            dma((2, 2)),
            dma((2,)),
            dma((3, team)),
            dma((3, team)),
            dma((3, team)),
            dma((3, team)),
        ],
        compiler_params=pltpu.CompilerParams(
            collective_id=0, has_side_effects=True, vmem_limit_bytes=64 * 1024 * 1024
        ),
    )(*arrays)
    pair_grad, proj_wgrad, gate_wgrad = pl.pallas_call(
        flush,
        out_shape=shapes,
        in_specs=[hbm] * 3,
        out_specs=(hbm, hbm, hbm),
        scratch_shapes=[pltpu.VMEM(a.shape, a.dtype) for a in shapes] + [dma((2, 3))],
        compiler_params=pltpu.CompilerParams(vmem_limit_bytes=64 * 1024 * 1024),
    )(*made)
    return pair_grad.reshape(tile, tile, width), proj_wgrad, gate_wgrad


def local(pair_norm, *rest):
    rows, cols = lax.axis_size("row"), lax.axis_size("col")
    tile_rows, tile_cols, width = pair_norm.shape
    hidden = rest[7].shape[0]
    team = rows * cols
    fits = (
        rows == cols == 4
        and tile_rows == tile_cols
        and tile_rows % 16 == 0
        and tile_rows <= 32
        and hidden == width
        and width == 128
    )
    return (fused if fits else plain)(pair_norm, *rest)


def solution(mesh):
    placed = (
        P(("groups", "row"), "col", None),
        P(("groups", "row"), "col"),
        P(("groups", "row"), "col", None),
        P(("groups", "row"), "col"),
        P(("groups", "row"), "col", None),
        P("groups"),
        P(),
        P(),
        P(),
        P(),
        P(),
    )
    return jax.shard_map(
        local,
        mesh=mesh,
        in_specs=placed,
        out_specs=(P(("groups", "row"), "col", None), P("groups", None), P("groups", None)),
        check_vma=False,
    )
```
